1024 devices in a mesh: dp: 64 (over z, core), tensor: 16 (over x, y).
Axes of the slice: x: 4, y: 4, z: 32, core: 2. Of those that a mesh axis runs over, the one named last changes fastest.
Arguments:
- x_quant: bfloat16 [384, 8192], P('tensor', 'dp'), may hold values from -6 to 6
- x_scale: float32 [16, 64], P('tensor', 'dp'), may hold values from 0.25 to 4
- x_outlier: int32 [16, 64], P('tensor', 'dp'), may hold values 0 or 1
- x_correction: bfloat16 [384, 8192], P('tensor', 'dp'), may hold values from -12 to 12
- g_quant: bfloat16 [384, 8192], P('tensor', 'dp'), may hold values from -6 to 6
- g_scale: float32 [16, 64], P('tensor', 'dp'), may hold values from 0.25 to 4
- g_outlier: int32 [16, 64], P('tensor', 'dp'), may hold values 0 or 1
- g_correction: bfloat16 [384, 8192], P('tensor', 'dp'), may hold values from -12 to 12
- gate_pre: bfloat16 [384, 26624], P('dp', 'tensor'), may hold values from -8 to 8
- up_pre: bfloat16 [384, 26624], P('dp', 'tensor'), may hold values from -6 to 6
- w_gate: bfloat16 [8192, 26624], P('dp', 'tensor'), may hold values from -0.0625 to 0.0625
- w_up: bfloat16 [8192, 26624], P('dp', 'tensor'), may hold values from -0.0625 to 0.0625
- w_down: bfloat16 [26624, 8192], P('tensor', 'dp'), may hold values from -0.0625 to 0.0625
Outputs:
- grad_input: bfloat16 [384, 8192], P('tensor', 'dp')
- grad_gate_weight: bfloat16 [8192, 26624], P('dp', 'tensor')
- grad_up_weight: bfloat16 [8192, 26624], P('dp', 'tensor')
- grad_down_weight: bfloat16 [26624, 8192], P('tensor', 'dp')
The draws below stay inside these ranges and needn't reach their ends.
All inputs are finite; a program needn't handle non-finite values. No bound on the sum of `x_outlier` or of `g_outlier` on one device may be relied on, other than what follows from the above.
Results may differ from the reference program's by a relative error of at most 0.0064.
Values may be sent and summed in bfloat16 or wider, within the bound.
A program may use at most 32 MiB of HBM per device.

```python
import math
import jax
import jax.numpy as jnp

D = 8192
FF = 26624
BLK_C = 128
TOK_DEV = 24
TOKENS = 384
N_TENSOR = 16


def with_ends(entries, rng, low, high):
    extent = entries.shape
    index_at = [jax.random.randint(jax.random.fold_in(rng, axis), (), 0, extent[axis]) for axis in range(len(extent))]
    entries = entries.at[tuple(index_at)].set(low)
    longest = extent.index(max(extent))
    index_at[longest] = (index_at[longest] + 1) % extent[longest]
    return entries.at[tuple(index_at)].set(high)


def shard_levels(own_key, shape, split, low, high):
    level, own = 1.0, jax.random.fold_in(own_key, 6)
    for axis_at, shards_of in split:
        draws = jnp.exp(jax.random.uniform(jax.random.fold_in(own, axis_at), (shards_of,), jnp.float32, low / len(split), high / len(split)))
        level = level * jnp.repeat(draws, shape[axis_at] // shards_of).reshape([-1 if axis == axis_at else 1 for axis in range(len(shape))])
    return level


def scatter_about(stream_key, shape, width, reach, split=(), held_as=jnp.bfloat16):
    drawn = width * jax.random.normal(stream_key, shape, jnp.float32)
    if split:
        drawn = drawn * shard_levels(stream_key, shape, split, -0.22, 0.18)
    return jnp.clip(drawn, -reach, reach).astype(held_as)


def setup_inputs(seed: int = 0) -> dict:
    arg_keys = jax.random.split(jax.random.key(seed), 14)
    x_quant = scatter_about(arg_keys[0], (TOKENS, D), 1.0, 6.0, ((0, 16), (1, 64)))
    x_scale = jnp.clip(jnp.exp(math.log(4.0) - 2.7725887 * jax.random.uniform(arg_keys[1], (N_TENSOR, D // BLK_C), jnp.float32) ** shard_levels(arg_keys[1], (N_TENSOR, D // BLK_C), ((0, 16), (1, 64)), -0.2, 0.2)), 0.25, 4.0)
    x_outlier = with_ends((jax.random.randint(arg_keys[2], (N_TENSOR, D // BLK_C), 0, 4) < 1).astype(jnp.int32), jax.random.fold_in(arg_keys[2], 1), 0, 1)
    x_correction = scatter_about(arg_keys[3], (TOKENS, D), 3.0, 12.0, ((0, 16), (1, 64)))
    g_quant = scatter_about(arg_keys[4], (TOKENS, D), 1.0, 6.0, ((0, 16), (1, 64)))
    g_scale = jnp.clip(jnp.exp(math.log(4.0) - 2.7725887 * jax.random.uniform(arg_keys[5], (N_TENSOR, D // BLK_C), jnp.float32) ** shard_levels(arg_keys[5], (N_TENSOR, D // BLK_C), ((0, 16), (1, 64)), -0.2, 0.2)), 0.25, 4.0)
    g_outlier = with_ends((jax.random.randint(arg_keys[6], (N_TENSOR, D // BLK_C), 0, 4) < 1).astype(jnp.int32), jax.random.fold_in(arg_keys[6], 1), 0, 1)
    g_correction = scatter_about(arg_keys[7], (TOKENS, D), 3.0, 12.0, ((0, 16), (1, 64)))
    gate_pre = scatter_about(arg_keys[8], (TOKENS, FF), 1.5, 8.0, ((0, 64), (1, 16)))
    up_pre = scatter_about(arg_keys[9], (TOKENS, FF), 1.0, 6.0, ((0, 64), (1, 16)))
    w_gate = scatter_about(arg_keys[10], (D, FF), D ** -0.5, 0.0625, ((0, 64), (1, 16)))
    w_up = scatter_about(arg_keys[11], (D, FF), D ** -0.5, 0.0625, ((0, 64), (1, 16)))
    w_down = scatter_about(arg_keys[12], (FF, D), D ** -0.5, 0.0625, ((0, 16), (1, 64)))
    return {"x_quant": x_quant, "x_scale": x_scale, "x_outlier": x_outlier, "x_correction": x_correction, "g_quant": g_quant, "g_scale": g_scale, "g_outlier": g_outlier, "g_correction": g_correction, "gate_pre": gate_pre, "up_pre": up_pre, "w_gate": w_gate, "w_up": w_up, "w_down": w_down}


def expand(block_values):
    return jnp.repeat(jnp.repeat(block_values, TOK_DEV, axis=0), BLK_C, axis=1)


def dequantize(quant, block_scale, outlier, correction):
    values = expand(block_scale) * quant.astype(jnp.float32) + expand(outlier.astype(jnp.float32)) * correction.astype(jnp.float32)
    return values.astype(jnp.bfloat16)


def reference(x_quant, x_scale, x_outlier, x_correction, g_quant, g_scale, g_outlier, g_correction, gate_pre, up_pre, w_gate, w_up, w_down):
    inputs = dequantize(x_quant, x_scale, x_outlier, x_correction)
    out_grad = dequantize(g_quant, g_scale, g_outlier, g_correction)
    hidden_grad = jnp.dot(out_grad, w_down.T, preferred_element_type=jnp.float32)
    gate_val = gate_pre.astype(jnp.float32)
    up_val = up_pre.astype(jnp.float32)
    sigmoid_gate = jax.nn.sigmoid(gate_val)
    silu_gate = gate_val * sigmoid_gate
    hidden = (silu_gate * up_val).astype(jnp.bfloat16)
    up_grad = (hidden_grad * silu_gate).astype(jnp.bfloat16)
    gate_grad = (hidden_grad * up_val * sigmoid_gate * (1.0 + gate_val * (1.0 - sigmoid_gate))).astype(jnp.bfloat16)
    grad_down_weight = jnp.dot(hidden.T, out_grad, preferred_element_type=jnp.float32).astype(jnp.bfloat16)
    grad_gate_weight = jnp.dot(inputs.T, gate_grad, preferred_element_type=jnp.float32).astype(jnp.bfloat16)
    grad_up_weight = jnp.dot(inputs.T, up_grad, preferred_element_type=jnp.float32).astype(jnp.bfloat16)
    grad_input = (jnp.dot(gate_grad, w_gate.T, preferred_element_type=jnp.float32) + jnp.dot(up_grad, w_up.T, preferred_element_type=jnp.float32)).astype(jnp.bfloat16)
    return grad_input, grad_gate_weight, grad_up_weight, grad_down_weight
```

```python
import jax
import jax.numpy as jnp
from jax import lax
from jax.experimental import pallas as pl
from jax.experimental.pallas import tpu as pltpu
from jax.sharding import PartitionSpec as P

MESH = pl.DeviceIdType.MESH
F32, BF16 = jnp.float32, jnp.bfloat16

NZ, STRIDE = 32, 4
NK = NZ // STRIDE
NT = 16
J = 13
ROWS = 192
CH = 80
FLAT = NZ * CH
CLS = NK * CH
HALF = CLS // 2
GCH = 2 * CH
GCLS = NK * GCH
GHALF = GCLS // 2
XY = 48


def rows_of(start, size, align=16):
    return pl.ds(pl.multiple_of(start, align), size)


def kernel(
    xs, xo, gs, go, xq, xc, gq, gc, gate, up, wd, wg, wu,
    gin, dgate, dup, ddown,
    xyb, tmp48, u4, xg, xot, og2, ogall, wd2, wgv, wuv,
    gpack, gbuf, tt, tg, tu, coef_a, coef_b, hid_o, hid_s,
    hf, hp, r1a, r1b, r1h, sb, sown, r2, ha,
    gu_o, gu_s, part, rs_src, rs_dst, fin, o_gate, o_up, o_down,
    loc_sem, sib_s, sib_r, xy_s, xy_r, gch_s, gch_r, glo_s, glo_r,
    r1_s, r1_r, r2_s, r2_r, a1_s, a1_r, a2_s, a2_r, rs_s, rs_r,
):
    dp, t = lax.axis_index("dp"), lax.axis_index("tensor")
    z, c = dp // 2, lax.rem(dp, 2)
    k0, cls = z // STRIDE, lax.rem(z, STRIDE)

    def zdev(d):
        return (lax.rem(dp + 2 * d + 2 * NZ, 2 * NZ), t)

    def tdev(i):
        return (dp, lax.rem(t + i, NT))

    sib = (dp + 1 - 2 * c, t)

    def rcopy(src, dst, ss, rs, dev):
        return pltpu.make_async_remote_copy(
            src_ref=src, dst_ref=dst, send_sem=ss, recv_sem=rs, device_id=dev, device_id_type=MESH
        )

    barrier = pltpu.get_barrier_semaphore()
    peers = [zdev(d) for d in (1, -1, 2, -2)] + [zdev(STRIDE * i) for i in range(1, NK)]
    peers += [sib] + [tdev(i) for i in range(1, NT)]
    for peer in peers:
        pl.semaphore_signal(barrier, inc=1, device_id=peer, device_id_type=MESH)

    loc = [
        pltpu.make_async_copy(wd, wd2.at[:, pl.ds(0, 128)], loc_sem.at[0]),
        pltpu.make_async_copy(wg, wgv, loc_sem.at[1]),
        pltpu.make_async_copy(wu, wuv, loc_sem.at[2]),
    ]
    for copy in loc:
        copy.start()

    fin[0] = xs[0, 0] * xq[...].astype(F32) + xo[0, 0].astype(F32) * xc[...].astype(F32)
    fin[1] = gs[0, 0] * gq[...].astype(F32) + go[0, 0].astype(F32) * gc[...].astype(F32)
    for a in range(2):
        for p in range(2):
            for h in range(2):
                tmp48[0, 24 * a + 12 * p + 6 * h : 24 * a + 12 * p + 6 * h + 6, :] = fin[
                    a, 12 * h + 6 * p : 12 * h + 6 * p + 6, :
                ]
    xyb[t] = tmp48[0].astype(BF16)

    gpack[...] = jnp.zeros_like(gpack)
    gate_val, up_val = gate[...].astype(F32), up[...].astype(F32)
    for j in range(J):
        gpack[6 * j : 6 * j + 6, :] = gate_val[:, 128 * j : 128 * j + 128]
        gpack[CH + 6 * j : CH + 6 * j + 6, :] = up_val[:, 128 * j : 128 * j + 128]

    def gslot(k):
        return gbuf.at[rows_of(GCLS * cls + GCH * k, GCH)]

    gbuf[rows_of(GCLS * cls + GCH * k0, GCH), :] = gpack[...].astype(BF16)
    pl.semaphore_wait(barrier, len(peers))

    xy = [
        rcopy(xyb.at[t], xyb.at[t], xy_s.at[i - 1], xy_r.at[i - 1], tdev(i))
        for i in (10, 5, 6, 7, 9, 11, 2, 8, 14, 13, 3, 1, 15, 4, 12)
    ]
    for copy in xy:
        copy.start()
    wd_copy = rcopy(wd, wd2.at[:, pl.ds(128, 128)], sib_s.at[0], sib_r.at[0], sib)
    wd_copy.start()

    def chain(s):
        kr, kl = lax.rem(k0 + NK - s + 1, NK), lax.rem(k0 + s - 1, NK)
        out = [rcopy(gslot(kr), gslot(kr), gch_s.at[s - 1], gch_r.at[s - 1], zdev(STRIDE))]
        if s < NK // 2:
            at = NK // 2 + s - 1
            out.append(rcopy(gslot(kl), gslot(kl), gch_s.at[at], gch_r.at[at], zdev(-STRIDE)))
        return out

    chains = [chain(s) for s in range(1, NK // 2 + 1)]
    for copy in chains[0]:
        copy.start()

    def chain_step(s):
        for copy in chains[s - 1]:
            copy.wait_recv()
        for copy in chains[s]:
            copy.start()

    for copy in xy:
        copy.wait_recv()
    for i in range(NT):
        tmp48[i % 4] = xyb[i].astype(F32)
        for a in range(4):
            u4[a, 12 * i : 12 * i + 12, :] = tmp48[i % 4, 12 * a : 12 * a + 12, :]
    for a in range(4):
        xg[a] = u4[a].astype(BF16)
    og_copy = rcopy(xg.at[3 - c], og2.at[:, pl.ds(128, 128)], sib_s.at[1], sib_r.at[1], sib)
    og_copy.start()
    og2[:, 0:128] = xg[2 + c]
    ogall[0:ROWS, :] = xg[2 + c]
    ogall[ROWS : 2 * ROWS, :] = xg[3 - c]
    tx = jnp.concatenate([u4[c], u4[1 - c]], axis=0)
    xot[...] = jnp.transpose(tx).astype(BF16)
    loc[0].wait()
    wd_copy.wait_recv()
    og_copy.wait_recv()

    hp[J * ROWS : FLAT, :] = jnp.zeros((FLAT - J * ROWS, 128), BF16)
    hf[J * ROWS : FLAT, :] = jnp.zeros((FLAT - J * ROWS, 128), F32)
    og_val = og2[...]
    for j in range(J):
        val = lax.dot_general(
            og_val, wd2[128 * j : 128 * j + 128, :], (((1,), (1,)), ((), ())),
            preferred_element_type=F32,
        )
        hf[ROWS * j : ROWS * (j + 1), :] = val
        hp[ROWS * j : ROWS * (j + 1), :] = val.astype(BF16)

    def near(d):
        return lax.rem(cls + d + STRIDE, STRIDE)

    def window(src, dst, cls_rows, sems_s, sems_r, towards):
        half = cls_rows // 2
        out = []
        for n, (d, off, size) in enumerate(
            ((2, 0, half), (-2, half, half), (1, 0, cls_rows), (-1, 0, cls_rows))
        ):
            base = cls_rows * (near(d) if towards else cls) + off
            view = src.at[rows_of(base, size)]
            land = view if dst is None else dst[n]
            out.append(rcopy(view, land, sems_s.at[n], sems_r.at[n], zdev(d)))
        return out

    r1 = window(hp, (r1h.at[rows_of(0, HALF)], r1h.at[rows_of(HALF, HALF)], r1a, r1b), CLS, r1_s, r1_r, True)
    for copy in r1:
        copy.start()
    chain_step(1)
    chain_step(2)
    for copy in r1:
        copy.wait_recv()

    def sum_window(i, _):
        at = rows_of(CH * i, CH)
        own = hf[rows_of(CLS * cls + CH * i, CH), :]
        total = own + r1a[at, :].astype(F32) + r1b[at, :].astype(F32) + r1h[at, :].astype(F32)
        sown[at, :] = total
        sb[at, :] = total.astype(BF16)
        return 0

    lax.fori_loop(0, NK, sum_window, 0)

    far = (4, 3, 5, 2, 6, 1, 7)

    def other(i):
        return lax.rem(k0 + i, NK)

    r2c = [
        rcopy(
            sb.at[rows_of(CH * other(i), CH)], r2.at[k0], r2_s.at[i - 1], r2_r.at[i - 1],
            zdev(STRIDE * i),
        )
        for i in far
    ]
    for copy in r2c:
        copy.start()
    chain_step(3)
    for copy in chains[3]:
        copy.wait_recv()
    glo = window(gbuf, None, GCLS, glo_s, glo_r, False)
    for copy in glo:
        copy.start()

    for copy in r2c:
        copy.wait_recv()
    total = sown[rows_of(CH * k0, CH), :]
    for i in range(1, NK):
        total = total + r2[other(i)].astype(F32)
    own_at = rows_of(CLS * cls + CH * k0, CH)
    ha[own_at, :] = total.astype(BF16)
    a1 = [
        rcopy(ha.at[own_at], ha.at[own_at], a1_s.at[i - 1], a1_r.at[i - 1], zdev(STRIDE * i))
        for i in far
    ]
    for copy in a1:
        copy.start()

    for copy in glo:
        copy.wait_recv()
    coef_a[J * ROWS : FLAT, :] = jnp.zeros((FLAT - J * ROWS, 128), F32)
    coef_b[J * ROWS : FLAT, :] = jnp.zeros((FLAT - J * ROWS, 128), F32)

    def factors(m, _):
        for q in range(8):
            start = GCLS * (q % STRIDE) + GCH * (q // STRIDE) + 2 * GCH * m
            tt[q] = gbuf[rows_of(start, GCH), :].astype(F32)
            for j in range(J):
                tg[j, 6 * q : 6 * q + 6, :] = tt[q, 6 * j : 6 * j + 6, :]
                tu[j, 6 * q : 6 * q + 6, :] = tt[q, CH + 6 * j : CH + 6 * j + 6, :]

        def tile(j, _):
            g, u = tg[j], tu[j]
            s = 1.0 / (1.0 + jnp.exp(-g))
            silu = g * s
            at = rows_of(ROWS * j + 48 * m, 48)
            hid_o[at, :] = (silu * u).astype(BF16)
            coef_a[at, :] = silu
            coef_b[at, :] = u * s * (1.0 + g * (1.0 - s))
            return 0

        lax.fori_loop(0, J, tile, 0)
        return 0

    lax.fori_loop(0, 4, factors, 0)
    hid_copy = rcopy(hid_o, hid_s, sib_s.at[2], sib_r.at[2], sib)
    hid_copy.start()
    hid_copy.wait_recv()

    def down(j, _):
        at = rows_of(ROWS * j, ROWS)
        both = jnp.concatenate([hid_o[at, :], hid_s[at, :]], axis=0)
        val = lax.dot_general(
            both, ogall[...], (((0,), (0,)), ((), ())), preferred_element_type=F32
        )
        o_down[rows_of(128 * j, 128), :] = val.astype(BF16)
        return 0

    lax.fori_loop(0, J, down, 0)
    out_down = pltpu.make_async_copy(o_down, ddown, loc_sem.at[3])
    out_down.start()

    for copy in a1:
        copy.wait_recv()
    a2 = window(ha, None, CLS, a2_s, a2_r, False)
    for copy in a2:
        copy.start()

    def grads(which, n):
        def body(i, _):
            at = rows_of(CLS * which + CH * i, CH)
            h = ha[at, :].astype(F32)
            gu_o[at, 0:128] = (h * coef_b[at, :]).astype(BF16)
            gu_o[at, 128:256] = (h * coef_a[at, :]).astype(BF16)
            return 0

        lax.fori_loop(0, NK, body, 0)
        at = rows_of(CLS * which, CLS)
        copy = rcopy(gu_o.at[at], gu_s.at[at], sib_s.at[3 + n], sib_r.at[3 + n], sib)
        copy.start()
        return copy

    gu = [grads(cls, 0)]
    a2[2].wait_recv()
    gu.append(grads(near(-1), 1))
    a2[3].wait_recv()
    gu.append(grads(near(1), 2))
    a2[0].wait_recv()
    a2[1].wait_recv()
    gu.append(grads(near(2), 3))

    loc[1].wait()
    loc[2].wait()

    def input_part(buf):
        acc = jnp.zeros((ROWS, 128), F32)
        for j in range(J):
            w = jnp.concatenate(
                [wgv[:, 128 * j : 128 * j + 128], wuv[:, 128 * j : 128 * j + 128]], axis=1
            )
            acc = acc + lax.dot_general(
                buf[ROWS * j : ROWS * (j + 1), :], w, (((1,), (1,)), ((), ())),
                preferred_element_type=F32,
            )
        return acc

    part[c] = input_part(gu_o)
    for copy in gu:
        copy.wait_recv()
    part[1 - c] = input_part(gu_s)
    for i in range(NT):
        for p in range(2):
            rs_src[i, 12 * p : 12 * p + 12, :] = part[p, 12 * i : 12 * i + 12, :]
    rs = [
        rcopy(
            rs_src.at[lax.rem(t + i, NT)], rs_dst.at[t], rs_s.at[i - 1], rs_r.at[i - 1], tdev(i)
        )
        for i in (10, 5, 6, 7, 9, 11, 2, 8, 14, 13, 3, 1, 15, 4, 12)
    ]
    for copy in rs:
        copy.start()
    rs_dst[t] = rs_src[t]

    for j in range(J):
        both = jnp.concatenate(
            [gu_o[ROWS * j : ROWS * (j + 1), :], gu_s[ROWS * j : ROWS * (j + 1), :]], axis=0
        )
        val = jnp.dot(xot[...], both, preferred_element_type=F32).astype(BF16)
        o_gate[:, 128 * j : 128 * j + 128] = val[:, 0:128]
        o_up[:, 128 * j : 128 * j + 128] = val[:, 128:256]
    outs = [
        pltpu.make_async_copy(o_gate, dgate, loc_sem.at[4]),
        pltpu.make_async_copy(o_up, dup, loc_sem.at[5]),
    ]
    for copy in outs:
        copy.start()

    sends = xy + [wd_copy, og_copy] + sum(chains, []) + r1 + r2c + glo + a1 + [hid_copy] + a2 + gu
    for copy in sends:
        copy.wait_send()
    for copy in rs:
        copy.wait()
    total = rs_dst[0]
    for i in range(1, NT):
        total = total + rs_dst[i]
    fin[0] = total
    for p in range(2):
        for h in range(2):
            fin[1, 12 * h + 6 * p : 12 * h + 6 * p + 6, :] = fin[
                0, 12 * p + 6 * h : 12 * p + 6 * h + 6, :
            ]
    gin[...] = fin[1].astype(BF16)
    out_down.wait()
    for copy in outs:
        copy.wait()


def on_device(
    x_quant, x_scale, x_outlier, x_correction, g_quant, g_scale, g_outlier, g_correction,
    gate_pre, up_pre, w_gate, w_up, w_down,
):
    vmem = pl.BlockSpec(memory_space=pltpu.VMEM)
    smem = pl.BlockSpec(memory_space=pltpu.SMEM)
    anywhere = pl.BlockSpec(memory_space=pl.ANY)
    v, dma = pltpu.VMEM, pltpu.SemaphoreType.DMA
    return pl.pallas_call(
        kernel,
        name="ffn_backward",
        out_shape=(
            jax.ShapeDtypeStruct((24, 128), BF16),
            jax.ShapeDtypeStruct((128, 128 * J), BF16),
            jax.ShapeDtypeStruct((128, 128 * J), BF16),
            jax.ShapeDtypeStruct((128 * J, 128), BF16),
        ),
        in_specs=[smem] * 4 + [vmem] * 6 + [anywhere] * 3,
        out_specs=(vmem, anywhere, anywhere, anywhere),
        scratch_shapes=[
            v((NT, XY, 128), BF16),
            v((4, XY, 128), F32),
            v((4, ROWS, 128), F32),
            v((4, ROWS, 128), BF16),
            v((128, 2 * ROWS), BF16),
            v((ROWS, 256), BF16),
            v((2 * ROWS, 128), BF16),
            v((128 * J, 256), BF16),
            v((128, 128 * J), BF16),
            v((128, 128 * J), BF16),
            v((GCH, 128), F32),
            v((NZ * GCH, 128), BF16),
            v((8, GCH, 128), F32),
            v((J, 48, 128), F32),
            v((J, 48, 128), F32),
            v((FLAT, 128), F32),
            v((FLAT, 128), F32),
            v((FLAT, 128), BF16),
            v((FLAT, 128), BF16),
            v((FLAT, 128), F32),
            v((FLAT, 128), BF16),
            v((CLS, 128), BF16),
            v((CLS, 128), BF16),
            v((CLS, 128), BF16),
            v((CLS, 128), BF16),
            v((CLS, 128), F32),
            v((NK, CH, 128), BF16),
            v((FLAT, 128), BF16),
            v((FLAT, 256), BF16),
            v((FLAT, 256), BF16),
            v((2, ROWS, 128), F32),
            v((NT, 24, 128), F32),
            v((NT, 24, 128), F32),
            v((2, 24, 128), F32),
            v((128, 128 * J), BF16),
            v((128, 128 * J), BF16),
            v((128 * J, 128), BF16),
            dma((6,)),
            dma((7,)), dma((7,)),
            dma((NT - 1,)), dma((NT - 1,)),
            dma((NK - 1,)), dma((NK - 1,)),
            dma((4,)), dma((4,)),
            dma((4,)), dma((4,)),
            dma((NK - 1,)), dma((NK - 1,)),
            dma((NK - 1,)), dma((NK - 1,)),
            dma((4,)), dma((4,)),
            dma((NT - 1,)), dma((NT - 1,)),
        ],
        compiler_params=pltpu.CompilerParams(
            collective_id=0, has_side_effects=True, vmem_limit_bytes=48 * 1024 * 1024
        ),
        cost_estimate=pl.CostEstimate(
            flops=1_200_000_000, bytes_accessed=8_000_000, transcendentals=400_000
        ),
    )(
        x_scale, x_outlier, g_scale, g_outlier, x_quant, x_correction, g_quant, g_correction,
        gate_pre, up_pre, w_down, w_gate, w_up,
    )


def solution(mesh):
    both = P("tensor", "dp")
    return jax.shard_map(
        on_device,
        mesh=mesh,
        in_specs=(both,) * 8 + (P("dp", "tensor"),) * 4 + (both,),
        out_specs=(both, P("dp", "tensor"), P("dp", "tensor"), both),
        check_vma=False,
    )
```

```python
import jax
import jax.numpy as jnp
from jax import lax
from jax.experimental import pallas as pl
from jax.experimental.pallas import tpu as pltpu
from jax.sharding import PartitionSpec as P

MESH = pl.DeviceIdType.MESH
F32, BF16 = jnp.float32, jnp.bfloat16

NZ, STRIDE = 32, 4
NK = NZ // STRIDE
NT = 16
J = 13
ROWS = 192
CH = 80
FLAT = NZ * CH
CLS = NK * CH
GCH = 2 * CH
GCLS = NK * GCH
XY = 48


def rows_of(start, size, align=16):
    return pl.ds(pl.multiple_of(start, align), size)


def kernel(
    xs_in, xo_in, gs_in, go_in, xq_in, xc_in, gq_in, gc_in, gate_in, up_in, wd, wg, wu,
    gin, dgate, dup, ddown,
    xs, xo, gs, go, xq, xc, gq, gc, gate, up,
    xyb, tmp48, u4, xg, xot, og2, ogall, wd2, wgv, wuv,
    gpack, gbuf, tt, tg, tu, coef_a, coef_b, hid_o, hid_s,
    hf, hp, r1b, r2s, r2r, ha,
    gu_o, gu_s, part, rs_src, rs_dst, fin, o_in, o_gate, o_up, o_down,
    in_sem, loc_sem, sib_s, sib_r, xy_s, xy_r, gch_s, gch_r, glo_s, glo_r,
    r1_s, r1_r, r2_s, r2_r, a1_s, a1_r, a2_s, a2_r, gu_ss, gu_rs, rs_s, rs_r,
):
    dp, t = lax.axis_index("dp"), lax.axis_index("tensor")
    z, c = dp // 2, lax.rem(dp, 2)
    k0, cls = z // STRIDE, lax.rem(z, STRIDE)

    def zdev(d):
        return (lax.rem(dp + 2 * d + 2 * NZ, 2 * NZ), t)

    def tdev(i):
        return (dp, lax.rem(t + i, NT))

    sib = (dp + 1 - 2 * c, t)

    def rcopy(src, dst, ss, rs, dev):
        return pltpu.make_async_remote_copy(
            src_ref=src, dst_ref=dst, send_sem=ss, recv_sem=rs, device_id=dev, device_id_type=MESH
        )

    barrier = pltpu.get_barrier_semaphore()
    peers = [zdev(d) for d in (1, -1, 2, -2, STRIDE, -STRIDE)]
    peers += [sib] + [tdev(i) for i in range(1, NT)]
    for peer in peers:
        pl.semaphore_signal(barrier, inc=1, device_id=peer, device_id_type=MESH)

    loc = [
        pltpu.make_async_copy(wd, wd2.at[:, pl.ds(0, 128)], loc_sem.at[0]),
        pltpu.make_async_copy(wg, wgv, loc_sem.at[1]),
        pltpu.make_async_copy(wu, wuv, loc_sem.at[2]),
    ]
    small = [
        pltpu.make_async_copy(src, dst, in_sem.at[n])
        for n, (src, dst) in enumerate(
            (
                (xq_in, xq), (xc_in, xc), (gq_in, gq), (gc_in, gc), (xs_in, xs), (xo_in, xo),
                (gs_in, gs), (go_in, go), (gate_in, gate), (up_in, up),
            )
        )
    ]
    for copy in small + loc:
        copy.start()
    for copy in small:
        copy.wait()

    fin[0] = xs[0, 0] * xq[...].astype(F32) + xo[0, 0].astype(F32) * xc[...].astype(F32)
    fin[1] = gs[0, 0] * gq[...].astype(F32) + go[0, 0].astype(F32) * gc[...].astype(F32)
    for a in range(2):
        for p in range(2):
            for h in range(2):
                tmp48[0, 24 * a + 12 * p + 6 * h : 24 * a + 12 * p + 6 * h + 6, :] = fin[
                    a, 12 * h + 6 * p : 12 * h + 6 * p + 6, :
                ]
    xyb[t] = tmp48[0].astype(BF16)

    def near(d):
        return lax.rem(cls + d + STRIDE, STRIDE)

    def k_of(d):
        return lax.rem(z + d + NZ, NZ) // STRIDE

    class Gather:
        which = (0, -1, -2, -3, -4, 1, 2, 3)
        towards = (1, -1, -2)

        def __init__(self, buf, ch, chain_s, chain_r, local_s, local_r):
            self.ch = ch

            def slot(n):
                return buf.at[self.rows(0, n)]

            def link(n, at, d):
                return rcopy(slot(n), slot(n), chain_s.at[at], chain_r.at[at], zdev(d))

            self.right = [link(n, n, STRIDE) for n in range(4)]
            self.left = [link((0, 5, 6)[n], 4 + n, -STRIDE) for n in range(3)]
            self.local = [
                [
                    rcopy(slot(n), slot(n), local_s.at[m, n], local_r.at[m, n], zdev(d))
                    for m, d in enumerate(self.towards)
                ]
                for n in range(NK)
            ]
            self.all = self.right + self.left + sum(self.local, [])

        def rows(self, d, n):
            k = lax.rem(k_of(d) + self.which[n] + NK, NK)
            return rows_of(NK * self.ch * near(d) + self.ch * k, self.ch)

        def begin(self):
            self.right[0].start()
            self.left[0].start()
            self.spread(0)

        def spread(self, n):
            for copy in self.local[n]:
                copy.start()

        def step(self, i):
            self.right[i - 1].wait_recv()
            if i < 4:
                self.right[i].start()
                self.left[i - 1].wait_recv()
            if i < 3:
                self.left[i].start()
            self.spread(i)
            if i < 4:
                self.spread(4 + i)

        def arrive(self, n):
            for copy in self.local[n]:
                copy.wait_recv()

    gpack[...] = jnp.zeros_like(gpack)
    gate_val, up_val = gate[...].astype(F32), up[...].astype(F32)
    for j in range(J):
        gpack[6 * j : 6 * j + 6, :] = gate_val[:, 128 * j : 128 * j + 128]
        gpack[CH + 6 * j : CH + 6 * j + 6, :] = up_val[:, 128 * j : 128 * j + 128]

    saved = Gather(gbuf, GCH, gch_s, gch_r, glo_s, glo_r)
    gbuf[saved.rows(0, 0), :] = gpack[...].astype(BF16)
    pl.semaphore_wait(barrier, len(peers))

    xy = [
        rcopy(xyb.at[t], xyb.at[t], xy_s.at[i - 1], xy_r.at[i - 1], tdev(i))
        for i in (10, 5, 6, 7, 9, 11, 2, 8, 14, 13, 3, 1, 15, 4, 12)
    ]
    for copy in xy:
        copy.start()
    wd_copy = rcopy(wd, wd2.at[:, pl.ds(128, 128)], sib_s.at[0], sib_r.at[0], sib)
    wd_copy.start()

    saved.begin()

    for copy in xy:
        copy.wait_recv()
    for i in range(NT):
        tmp48[i % 4] = xyb[i].astype(F32)
        for a in range(4):
            u4[a, 12 * i : 12 * i + 12, :] = tmp48[i % 4, 12 * a : 12 * a + 12, :]
    for a in range(4):
        xg[a] = u4[a].astype(BF16)
    og_copy = rcopy(xg.at[3 - c], og2.at[:, pl.ds(128, 128)], sib_s.at[1], sib_r.at[1], sib)
    og_copy.start()
    saved.step(1)
    og2[:, 0:128] = xg[2 + c]
    ogall[0:ROWS, :] = xg[2 + c]
    ogall[ROWS : 2 * ROWS, :] = xg[3 - c]
    tx = jnp.concatenate([u4[c], u4[1 - c]], axis=0)
    xot[...] = jnp.transpose(tx).astype(BF16)
    loc[0].wait()
    wd_copy.wait_recv()
    og_copy.wait_recv()

    hp[J * ROWS : FLAT, :] = jnp.zeros((FLAT - J * ROWS, 128), BF16)
    hf[J * ROWS : FLAT, :] = jnp.zeros((FLAT - J * ROWS, 128), F32)
    og_val = og2[...]
    for j in range(J):
        val = lax.dot_general(
            og_val, wd2[128 * j : 128 * j + 128, :], (((1,), (1,)), ((), ())),
            preferred_element_type=F32,
        )
        hf[ROWS * j : ROWS * (j + 1), :] = val
        hp[ROWS * j : ROWS * (j + 1), :] = val.astype(BF16)

    r1 = {}
    for off in (4, 5, 3, 6, 2, 7, 1, 0):
        for n, d in enumerate((1, -1, 2)):
            base = CLS * near(d) + CH * lax.rem(k_of(d) + off, NK)
            r1[off, n] = rcopy(
                hp.at[rows_of(base, CH)], r1b.at[n, off], r1_s.at[n, off], r1_r.at[n, off], zdev(d)
            )
            r1[off, n].start()

    def window_sum(off):
        total = hf[rows_of(CLS * cls + CH * lax.rem(k0 + off, NK), CH), :]
        for n in range(3):
            r1[off, n].wait_recv()
            total = total + r1b[n, off].astype(F32)
        return total

    saved.step(2)
    r2 = {}
    for i in range(1, 5):
        for w, off, d in ((0, 5 - i, STRIDE), (1, 4 + i, -STRIDE)):
            if w == 1 and i == 4:
                continue
            total = window_sum(off)
            if i > 1:
                r2[w, i - 1].wait_recv()
                total = total + r2r[w, i - 2].astype(F32)
            r2s[w, i - 1] = total.astype(BF16)
            r2[w, i] = rcopy(
                r2s.at[w, i - 1], r2r.at[w, i - 1], r2_s.at[w, i - 1], r2_r.at[w, i - 1], zdev(d)
            )
            r2[w, i].start()
        if i < 3:
            saved.step(2 + i)
    total = window_sum(0)
    r2[1, 3].wait_recv()
    total = total + r2r[1, 2].astype(F32)
    r2[0, 4].wait_recv()
    total = total + r2r[0, 3].astype(F32)
    back = Gather(ha, CH, a1_s, a1_r, a2_s, a2_r)
    ha[back.rows(0, 0), :] = total.astype(BF16)
    back.begin()

    for n in range(NK):
        saved.arrive(n)
    coef_a[J * ROWS : FLAT, :] = jnp.zeros((FLAT - J * ROWS, 128), F32)
    coef_b[J * ROWS : FLAT, :] = jnp.zeros((FLAT - J * ROWS, 128), F32)

    def factors(m, _):
        for q in range(8):
            start = GCLS * (q % STRIDE) + GCH * (q // STRIDE) + 2 * GCH * m
            tt[q] = gbuf[rows_of(start, GCH), :].astype(F32)
            for j in range(J):
                tg[j, 6 * q : 6 * q + 6, :] = tt[q, 6 * j : 6 * j + 6, :]
                tu[j, 6 * q : 6 * q + 6, :] = tt[q, CH + 6 * j : CH + 6 * j + 6, :]

        def tile(j, _):
            g, u = tg[j], tu[j]
            s = 1.0 / (1.0 + jnp.exp(-g))
            silu = g * s
            at = rows_of(ROWS * j + 48 * m, 48)
            hid_o[at, :] = (silu * u).astype(BF16)
            coef_a[at, :] = silu
            coef_b[at, :] = u * s * (1.0 + g * (1.0 - s))
            return 0

        lax.fori_loop(0, J, tile, 0)
        return 0

    lax.fori_loop(0, 4, factors, 0)
    hid_copy = rcopy(hid_o, hid_s, sib_s.at[2], sib_r.at[2], sib)
    hid_copy.start()
    back.step(1)
    hid_copy.wait_recv()

    def down(j, _):
        at = rows_of(ROWS * j, ROWS)
        both = jnp.concatenate([hid_o[at, :], hid_s[at, :]], axis=0)
        val = lax.dot_general(
            both, ogall[...], (((0,), (0,)), ((), ())), preferred_element_type=F32
        )
        o_down[rows_of(128 * j, 128), :] = val.astype(BF16)
        return 0

    lax.fori_loop(0, J, down, 0)

    outs = [pltpu.make_async_copy(o_down, ddown, loc_sem.at[3])]
    outs[0].start()

    gu = []

    def grads(d, n):
        at = back.rows(d, n)
        h = ha[at, :].astype(F32)
        gu_o[at, 0:128] = (h * coef_b[at, :]).astype(BF16)
        gu_o[at, 128:256] = (h * coef_a[at, :]).astype(BF16)
        m = len(gu)
        gu.append(rcopy(gu_o.at[at], gu_s.at[at], gu_ss.at[m], gu_rs.at[m], sib))
        gu[m].start()

    def arrived(n):
        for m, d in enumerate(back.towards):
            back.local[n][m].wait_recv()
            grads(-d, n)

    grads(0, 0)
    for n in (1, 5):
        grads(0, n)
    arrived(0)
    back.step(2)
    grads(0, 2)
    grads(0, 6)
    arrived(1)
    arrived(5)
    back.step(3)
    grads(0, 3)
    grads(0, 7)
    arrived(2)
    arrived(6)
    back.step(4)
    grads(0, 4)
    arrived(3)
    arrived(7)
    arrived(4)

    loc[1].wait()
    loc[2].wait()

    def input_part(buf):
        acc = jnp.zeros((ROWS, 128), F32)
        for j in range(J):
            w = jnp.concatenate(
                [wgv[:, 128 * j : 128 * j + 128], wuv[:, 128 * j : 128 * j + 128]], axis=1
            )
            acc = acc + lax.dot_general(
                buf[ROWS * j : ROWS * (j + 1), :], w, (((1,), (1,)), ((), ())),
                preferred_element_type=F32,
            )
        return acc

    part[c] = input_part(gu_o)
    for copy in gu:
        copy.wait_recv()
    part[1 - c] = input_part(gu_s)
    for i in range(NT):
        for p in range(2):
            rs_src[i, 12 * p : 12 * p + 12, :] = part[p, 12 * i : 12 * i + 12, :]
    rs = [
        rcopy(
            rs_src.at[lax.rem(t + i, NT)], rs_dst.at[t], rs_s.at[i - 1], rs_r.at[i - 1], tdev(i)
        )
        for i in (10, 5, 6, 7, 9, 11, 2, 8, 14, 13, 3, 1, 15, 4, 12)
    ]
    for copy in rs:
        copy.start()
    rs_dst[t] = rs_src[t]

    for j in range(J):
        both = jnp.concatenate(
            [gu_o[ROWS * j : ROWS * (j + 1), :], gu_s[ROWS * j : ROWS * (j + 1), :]], axis=0
        )
        val = jnp.dot(xot[...], both, preferred_element_type=F32).astype(BF16)
        o_gate[:, 128 * j : 128 * j + 128] = val[:, 0:128]
        o_up[:, 128 * j : 128 * j + 128] = val[:, 128:256]
    outs.append(pltpu.make_async_copy(o_gate, dgate, loc_sem.at[4]))
    outs.append(pltpu.make_async_copy(o_up, dup, loc_sem.at[5]))
    outs[1].start()
    outs[2].start()

    sends = xy + [wd_copy, og_copy, hid_copy] + saved.all + back.all + gu
    sends += list(r1.values()) + list(r2.values())
    for copy in sends:
        copy.wait_send()
    for copy in rs:
        copy.wait()
    total = rs_dst[0]
    for i in range(1, NT):
        total = total + rs_dst[i]
    fin[0] = total
    for p in range(2):
        for h in range(2):
            fin[1, 12 * h + 6 * p : 12 * h + 6 * p + 6, :] = fin[
                0, 12 * p + 6 * h : 12 * p + 6 * h + 6, :
            ]
    o_in[...] = fin[1].astype(BF16)
    outs.append(pltpu.make_async_copy(o_in, gin, loc_sem.at[6]))
    outs[3].start()
    for copy in outs:
        copy.wait()


def on_device(
    x_quant, x_scale, x_outlier, x_correction, g_quant, g_scale, g_outlier, g_correction,
    gate_pre, up_pre, w_gate, w_up, w_down,
):
    hbm = pl.BlockSpec(memory_space=pltpu.HBM)
    v, m, dma = pltpu.VMEM, pltpu.SMEM, pltpu.SemaphoreType.DMA
    return pl.pallas_call(
        kernel,
        name="ffn_backward",
        out_shape=(
            jax.ShapeDtypeStruct((24, 128), BF16),
            jax.ShapeDtypeStruct((128, 128 * J), BF16),
            jax.ShapeDtypeStruct((128, 128 * J), BF16),
            jax.ShapeDtypeStruct((128 * J, 128), BF16),
        ),
        in_specs=[hbm] * 13,
        out_specs=(hbm,) * 4,
        scratch_shapes=[
            m((1, 1), F32), m((1, 1), jnp.int32), m((1, 1), F32), m((1, 1), jnp.int32),
            v((24, 128), BF16), v((24, 128), BF16), v((24, 128), BF16), v((24, 128), BF16),
            v((6, 128 * J), BF16), v((6, 128 * J), BF16),
            v((NT, XY, 128), BF16),
            v((4, XY, 128), F32),
            v((4, ROWS, 128), F32),
            v((4, ROWS, 128), BF16),
            v((128, 2 * ROWS), BF16),
            v((ROWS, 256), BF16),
            v((2 * ROWS, 128), BF16),
            v((128 * J, 256), BF16),
            v((128, 128 * J), BF16),
            v((128, 128 * J), BF16),
            v((GCH, 128), F32),
            v((NZ * GCH, 128), BF16),
            v((8, GCH, 128), F32),
            v((J, 48, 128), F32),
            v((J, 48, 128), F32),
            v((FLAT, 128), F32),
            v((FLAT, 128), F32),
            v((FLAT, 128), BF16),
            v((FLAT, 128), BF16),
            v((FLAT, 128), F32),
            v((FLAT, 128), BF16),
            v((3, NK, CH, 128), BF16),
            v((2, 4, CH, 128), BF16),
            v((2, 4, CH, 128), BF16),
            v((FLAT, 128), BF16),
            v((FLAT, 256), BF16),
            v((FLAT, 256), BF16),
            v((2, ROWS, 128), F32),
            v((NT, 24, 128), F32),
            v((NT, 24, 128), F32),
            v((2, 24, 128), F32),
            v((24, 128), BF16),
            v((128, 128 * J), BF16),
            v((128, 128 * J), BF16),
            v((128 * J, 128), BF16),
            dma((10,)), dma((7,)),
            dma((3,)), dma((3,)),
            dma((NT - 1,)), dma((NT - 1,)),
            dma((NK - 1,)), dma((NK - 1,)),
            dma((3, NK)), dma((3, NK)),
            dma((3, NK)), dma((3, NK)),
            dma((2, 4)), dma((2, 4)),
            dma((NK - 1,)), dma((NK - 1,)),
            dma((3, NK)), dma((3, NK)),
            dma((NZ,)), dma((NZ,)),
            dma((NT - 1,)), dma((NT - 1,)),
        ],
        compiler_params=pltpu.CompilerParams(
            collective_id=0, has_side_effects=True, vmem_limit_bytes=63 * 1024 * 1024
        ),
        cost_estimate=pl.CostEstimate(
            flops=1_200_000_000, bytes_accessed=8_000_000, transcendentals=400_000
        ),
    )(
        x_scale, x_outlier, g_scale, g_outlier, x_quant, x_correction, g_quant, g_correction,
        gate_pre, up_pre, w_down, w_gate, w_up,
    )


def solution(mesh):
    both = P("tensor", "dp")
    return jax.shard_map(
        on_device,
        mesh=mesh,
        in_specs=(both,) * 8 + (P("dp", "tensor"),) * 4 + (both,),
        out_specs=(both, P("dp", "tensor"), P("dp", "tensor"), both),
        check_vma=False,
    )
```

```python
import jax
import jax.numpy as jnp
from jax import lax
from jax.experimental import pallas as pl
from jax.experimental.pallas import tpu as pltpu
from jax.sharding import PartitionSpec as P

MESH = pl.DeviceIdType.MESH
F32, BF16 = jnp.float32, jnp.bfloat16

NZ, STRIDE = 32, 4
NK = NZ // STRIDE
NT = 16
J = 13
ROWS = 192
CH = 80
FLAT = NZ * CH
CLS = NK * CH
GCH = 2 * CH
XY = 48


def rows_of(start, size, align=16):
    return pl.ds(pl.multiple_of(start, align), size)


def kernel(
    xs_in, xo_in, gs_in, go_in, xq_in, xc_in, gq_in, gc_in, gate_in, up_in, wd, wg, wu,
    gin, dgate, dup, ddown,
    xs, xo, gs, go, xq, xc, gq, gc, gate, up,
    xyb, tmp48, u4, xg, xot, og2, ogall, wd2, wgv, wuv,
    gpack, gbuf, tt, tg, tu, coef_a, coef_b, hid_o, hid_s,
    hf, hp, r1b, r2s, r2r, ha,
    gu_o, gu_s, part, rs_src, rs_dst, fin, o_in, o_gate, o_up, o_down,
    in_sem, loc_sem, sib_s, sib_r, xy_s, xy_r, gch_s, gch_r, glo_s, glo_r,
    r1_s, r1_r, r2_s, r2_r, a1_s, a1_r, a2_s, a2_r, gu_ss, gu_rs, rs_s, rs_r,
):
    dp, t = lax.axis_index("dp"), lax.axis_index("tensor")
    z, c = dp // 2, lax.rem(dp, 2)
    k0, cls = z // STRIDE, lax.rem(z, STRIDE)

    def zdev(d):
        return (lax.rem(dp + 2 * d + 2 * NZ, 2 * NZ), t)

    def tdev(i):
        return (dp, lax.rem(t + i, NT))

    sib = (dp + 1 - 2 * c, t)

    def rcopy(src, dst, ss, rs, dev):
        return pltpu.make_async_remote_copy(
            src_ref=src, dst_ref=dst, send_sem=ss, recv_sem=rs, device_id=dev, device_id_type=MESH
        )

    barrier = pltpu.get_barrier_semaphore()
    peers = [zdev(d) for d in (1, -1, 2, -2, STRIDE, -STRIDE)]
    peers += [sib] + [tdev(i) for i in range(1, NT)]
    for peer in peers:
        pl.semaphore_signal(barrier, inc=1, device_id=peer, device_id_type=MESH)

    loc = [
        pltpu.make_async_copy(wd, wd2.at[:, pl.ds(0, 128)], loc_sem.at[0]),
        pltpu.make_async_copy(wg, wgv, loc_sem.at[1]),
        pltpu.make_async_copy(wu, wuv, loc_sem.at[2]),
    ]
    small = [
        pltpu.make_async_copy(src, dst, in_sem.at[n])
        for n, (src, dst) in enumerate(
            (
                (xq_in, xq), (xc_in, xc), (gq_in, gq), (gc_in, gc), (xs_in, xs), (xo_in, xo),
                (gs_in, gs), (go_in, go), (gate_in, gate), (up_in, up),
            )
        )
    ]
    for copy in small + loc:
        copy.start()
    for copy in small:
        copy.wait()

    fin[0] = xs[0, 0] * xq[...].astype(F32) + xo[0, 0].astype(F32) * xc[...].astype(F32)
    fin[1] = gs[0, 0] * gq[...].astype(F32) + go[0, 0].astype(F32) * gc[...].astype(F32)
    for a in range(2):
        for p in range(2):
            for h in range(2):
                tmp48[0, 24 * a + 12 * p + 6 * h : 24 * a + 12 * p + 6 * h + 6, :] = fin[
                    a, 12 * h + 6 * p : 12 * h + 6 * p + 6, :
                ]
    xyb[t] = tmp48[0].astype(BF16)

    def near(d):
        return lax.rem(cls + d + STRIDE, STRIDE)

    def k_of(d):
        return lax.rem(z + d + NZ, NZ) // STRIDE

    class Gather:
        def __init__(self, buf, ch, stride, towards, chain_s, chain_r, local_s, local_r):
            self.ch, self.stride, self.towards = ch, stride, towards
            self.nk = nk = NZ // stride
            self.half = half = nk // 2
            self.which = tuple(range(0, -half - 1, -1)) + tuple(range(1, half))

            def slot(n):
                return buf.at[self.rows(0, n)]

            def link(n, at, d):
                return rcopy(slot(n), slot(n), chain_s.at[at], chain_r.at[at], zdev(d))

            self.right = [link(n, n, stride) for n in range(half)]
            self.left = [link(half + n if n else 0, half + n, -stride) for n in range(half - 1)]
            self.local = []
            for n in range(nk):
                if towards:
                    self.local.append(
                        [
                            rcopy(slot(n), slot(n), local_s.at[m, n], local_r.at[m, n], zdev(d))
                            for m, d in enumerate(towards)
                        ]
                    )
                else:
                    at = self.index(0, n)
                    to = (lax.rem(dp + 2 - 4 * lax.rem(at, 2) + 2 * NZ, 2 * NZ), t)
                    self.local.append(
                        [rcopy(slot(n), slot(n), local_s.at[n], local_r.at[at], to)]
                    )
            self.all = self.right + self.left + sum(self.local, [])

        def index(self, d, n):
            return lax.rem(lax.rem(z + d + NZ, NZ) // self.stride + self.which[n] + self.nk, self.nk)

        def rows(self, d, n):
            cls_at = lax.rem(lax.rem(z, self.stride) + d + self.stride, self.stride)
            return rows_of(self.ch * (self.nk * cls_at + self.index(d, n)), self.ch)

        def begin(self):
            self.right[0].start()
            self.left[0].start()
            self.spread(0)

        def spread(self, n):
            for copy in self.local[n]:
                copy.start()

        def step(self, i):
            half = self.half
            self.right[i - 1].wait_recv()
            if i < half:
                self.right[i].start()
                self.left[i - 1].wait_recv()
            if i < half - 1:
                self.left[i].start()
            self.spread(i)
            if i < half:
                self.spread(half + i)

        def arrive(self, n):
            for copy in self.local[n]:
                copy.wait_recv()

    gpack[...] = jnp.zeros_like(gpack)
    gate_val, up_val = gate[...].astype(F32), up[...].astype(F32)
    for j in range(J):
        gpack[6 * j : 6 * j + 6, :] = gate_val[:, 128 * j : 128 * j + 128]
        gpack[CH + 6 * j : CH + 6 * j + 6, :] = up_val[:, 128 * j : 128 * j + 128]

    saved = Gather(gbuf, GCH, 2, (), gch_s, gch_r, glo_s, glo_r)
    gbuf[saved.rows(0, 0), :] = gpack[...].astype(BF16)
    pl.semaphore_wait(barrier, len(peers))

    xy = [
        rcopy(xyb.at[t], xyb.at[t], xy_s.at[i - 1], xy_r.at[i - 1], tdev(i))
        for i in (10, 5, 6, 7, 9, 11, 2, 8, 14, 13, 3, 1, 15, 4, 12)
    ]
    for copy in xy:
        copy.start()
    wd_copy = rcopy(wd, wd2.at[:, pl.ds(128, 128)], sib_s.at[0], sib_r.at[0], sib)
    wd_copy.start()

    saved.begin()

    saved.step(1)
    for copy in xy:
        copy.wait_recv()
    for i in range(NT):
        tmp48[i % 4] = xyb[i].astype(F32)
        for a in range(4):
            u4[a, 12 * i : 12 * i + 12, :] = tmp48[i % 4, 12 * a : 12 * a + 12, :]
    for a in range(4):
        xg[a] = u4[a].astype(BF16)
    og_copy = rcopy(xg.at[3 - c], og2.at[:, pl.ds(128, 128)], sib_s.at[1], sib_r.at[1], sib)
    og_copy.start()
    og2[:, 0:128] = xg[2 + c]
    ogall[0:ROWS, :] = xg[2 + c]
    ogall[ROWS : 2 * ROWS, :] = xg[3 - c]
    tx = jnp.concatenate([u4[c], u4[1 - c]], axis=0)
    xot[...] = jnp.transpose(tx).astype(BF16)
    loc[0].wait()
    wd_copy.wait_recv()
    og_copy.wait_recv()
    saved.step(2)

    hp[J * ROWS : FLAT, :] = jnp.zeros((FLAT - J * ROWS, 128), BF16)
    hf[J * ROWS : FLAT, :] = jnp.zeros((FLAT - J * ROWS, 128), F32)
    og_val = og2[...]
    for j in range(J):
        val = lax.dot_general(
            og_val, wd2[128 * j : 128 * j + 128, :], (((1,), (1,)), ((), ())),
            preferred_element_type=F32,
        )
        hf[ROWS * j : ROWS * (j + 1), :] = val
        hp[ROWS * j : ROWS * (j + 1), :] = val.astype(BF16)

    r1 = {}
    for off in (4, 5, 3, 6, 2, 7, 1, 0):
        for n, d in enumerate((1, -1, 2)):
            base = CLS * near(d) + CH * lax.rem(k_of(d) + off, NK)
            r1[off, n] = rcopy(
                hp.at[rows_of(base, CH)], r1b.at[n, off], r1_s.at[n, off], r1_r.at[n, off], zdev(d)
            )
            r1[off, n].start()

    def window_sum(off):
        total = hf[rows_of(CLS * cls + CH * lax.rem(k0 + off, NK), CH), :]
        for n in range(3):
            r1[off, n].wait_recv()
            total = total + r1b[n, off].astype(F32)
        return total

    saved.step(3)
    r2 = {}
    for i in range(1, 5):
        for w, off, d in ((0, 5 - i, STRIDE), (1, 4 + i, -STRIDE)):
            if w == 1 and i == 4:
                continue
            total = window_sum(off)
            if i > 1:
                r2[w, i - 1].wait_recv()
                total = total + r2r[w, i - 2].astype(F32)
            r2s[w, i - 1] = total.astype(BF16)
            r2[w, i] = rcopy(
                r2s.at[w, i - 1], r2r.at[w, i - 1], r2_s.at[w, i - 1], r2_r.at[w, i - 1], zdev(d)
            )
            r2[w, i].start()
        saved.step(3 + i)
    total = window_sum(0)
    r2[1, 3].wait_recv()
    total = total + r2r[1, 2].astype(F32)
    r2[0, 4].wait_recv()
    total = total + r2r[0, 3].astype(F32)
    back = Gather(ha, CH, STRIDE, (1, -1, -2), a1_s, a1_r, a2_s, a2_r)
    ha[back.rows(0, 0), :] = total.astype(BF16)
    back.begin()
    saved.step(8)

    back.step(1)
    for n in range(NZ // 2):
        saved.arrive(n)
    coef_a[J * ROWS : FLAT, :] = jnp.zeros((FLAT - J * ROWS, 128), F32)
    coef_b[J * ROWS : FLAT, :] = jnp.zeros((FLAT - J * ROWS, 128), F32)

    def factors(m, _):
        for q in range(8):
            start = GCH * (NZ // 2 * (q % 2) + q // 2 + 4 * m)
            tt[q] = gbuf[rows_of(start, GCH), :].astype(F32)
            for j in range(J):
                tg[j, 6 * q : 6 * q + 6, :] = tt[q, 6 * j : 6 * j + 6, :]
                tu[j, 6 * q : 6 * q + 6, :] = tt[q, CH + 6 * j : CH + 6 * j + 6, :]

        def tile(j, _):
            g, u = tg[j], tu[j]
            s = 1.0 / (1.0 + jnp.exp(-g))
            silu = g * s
            at = rows_of(ROWS * j + 48 * m, 48)
            hid_o[at, :] = (silu * u).astype(BF16)
            coef_a[at, :] = silu
            coef_b[at, :] = u * s * (1.0 + g * (1.0 - s))
            return 0

        lax.fori_loop(0, J, tile, 0)
        return 0

    lax.fori_loop(0, 4, factors, 0)
    hid_copy = rcopy(hid_o, hid_s, sib_s.at[2], sib_r.at[2], sib)
    hid_copy.start()
    gu = []

    def grads(d, n):
        at = back.rows(d, n)
        h = ha[at, :].astype(F32)
        gu_o[at, 0:128] = (h * coef_b[at, :]).astype(BF16)
        gu_o[at, 128:256] = (h * coef_a[at, :]).astype(BF16)
        m = len(gu)
        gu.append(rcopy(gu_o.at[at], gu_s.at[at], gu_ss.at[m], gu_rs.at[m], sib))
        gu[m].start()

    def arrived(n):
        for m, d in enumerate(back.towards):
            back.local[n][m].wait_recv()
            grads(-d, n)

    grads(0, 0)
    for n in (1, 5):
        grads(0, n)
    arrived(0)
    back.step(2)
    hid_copy.wait_recv()

    def down(j, _):
        at = rows_of(ROWS * j, ROWS)
        both = jnp.concatenate([hid_o[at, :], hid_s[at, :]], axis=0)
        val = lax.dot_general(
            both, ogall[...], (((0,), (0,)), ((), ())), preferred_element_type=F32
        )
        o_down[rows_of(128 * j, 128), :] = val.astype(BF16)
        return 0

    lax.fori_loop(0, J, down, 0)

    outs = [pltpu.make_async_copy(o_down, ddown, loc_sem.at[3])]
    outs[0].start()

    grads(0, 2)
    grads(0, 6)
    arrived(1)
    arrived(5)
    back.step(3)
    grads(0, 3)
    grads(0, 7)
    arrived(2)
    arrived(6)
    back.step(4)
    grads(0, 4)
    arrived(3)
    arrived(7)
    arrived(4)

    loc[1].wait()
    loc[2].wait()

    def input_part(buf):
        acc = jnp.zeros((ROWS, 128), F32)
        for j in range(J):
            w = jnp.concatenate(
                [wgv[:, 128 * j : 128 * j + 128], wuv[:, 128 * j : 128 * j + 128]], axis=1
            )
            acc = acc + lax.dot_general(
                buf[ROWS * j : ROWS * (j + 1), :], w, (((1,), (1,)), ((), ())),
                preferred_element_type=F32,
            )
        return acc

    part[c] = input_part(gu_o)
    for copy in gu:
        copy.wait_recv()
    part[1 - c] = input_part(gu_s)
    for i in range(NT):
        for p in range(2):
            rs_src[i, 12 * p : 12 * p + 12, :] = part[p, 12 * i : 12 * i + 12, :]
    rs = [
        rcopy(
            rs_src.at[lax.rem(t + i, NT)], rs_dst.at[t], rs_s.at[i - 1], rs_r.at[i - 1], tdev(i)
        )
        for i in (10, 5, 6, 7, 9, 11, 2, 8, 14, 13, 3, 1, 15, 4, 12)
    ]
    for copy in rs:
        copy.start()
    rs_dst[t] = rs_src[t]

    for j in range(J):
        both = jnp.concatenate(
            [gu_o[ROWS * j : ROWS * (j + 1), :], gu_s[ROWS * j : ROWS * (j + 1), :]], axis=0
        )
        val = jnp.dot(xot[...], both, preferred_element_type=F32).astype(BF16)
        o_gate[:, 128 * j : 128 * j + 128] = val[:, 0:128]
        o_up[:, 128 * j : 128 * j + 128] = val[:, 128:256]
    outs.append(pltpu.make_async_copy(o_gate, dgate, loc_sem.at[4]))
    outs.append(pltpu.make_async_copy(o_up, dup, loc_sem.at[5]))
    outs[1].start()
    outs[2].start()

    sends = xy + [wd_copy, og_copy, hid_copy] + saved.all + back.all + gu
    sends += list(r1.values()) + list(r2.values())
    for copy in sends:
        copy.wait_send()
    for copy in rs:
        copy.wait()
    total = rs_dst[0]
    for i in range(1, NT):
        total = total + rs_dst[i]
    fin[0] = total
    for p in range(2):
        for h in range(2):
            fin[1, 12 * h + 6 * p : 12 * h + 6 * p + 6, :] = fin[
                0, 12 * p + 6 * h : 12 * p + 6 * h + 6, :
            ]
    o_in[...] = fin[1].astype(BF16)
    outs.append(pltpu.make_async_copy(o_in, gin, loc_sem.at[6]))
    outs[3].start()
    for copy in outs:
        copy.wait()


def deliver_kernel(a, b, c, d, a_out, b_out, c_out, d_out, sem):
    copies = [
        pltpu.make_async_copy(src, dst, sem.at[n])
        for n, (src, dst) in enumerate(((b, b_out), (c, c_out), (d, d_out), (a, a_out)))
    ]
    for copy in copies:
        copy.start()
    for copy in copies:
        copy.wait()


def deliver(*results):
    hbm = pl.BlockSpec(memory_space=pltpu.HBM)
    return pl.pallas_call(
        deliver_kernel,
        name="deliver",
        out_shape=tuple(jax.ShapeDtypeStruct(r.shape, r.dtype) for r in results),
        in_specs=[hbm] * 4,
        out_specs=(hbm,) * 4,
        scratch_shapes=[pltpu.SemaphoreType.DMA((4,))],
        compiler_params=pltpu.CompilerParams(vmem_limit_bytes=63 * 1024 * 1024),
    )(*results)


def on_device(
    x_quant, x_scale, x_outlier, x_correction, g_quant, g_scale, g_outlier, g_correction,
    gate_pre, up_pre, w_gate, w_up, w_down,
):
    hbm = pl.BlockSpec(memory_space=pltpu.HBM)
    v, m, dma = pltpu.VMEM, pltpu.SMEM, pltpu.SemaphoreType.DMA
    results = pl.pallas_call(
        kernel,
        name="ffn_backward",
        out_shape=(
            jax.ShapeDtypeStruct((24, 128), BF16),
            jax.ShapeDtypeStruct((128, 128 * J), BF16),
            jax.ShapeDtypeStruct((128, 128 * J), BF16),
            jax.ShapeDtypeStruct((128 * J, 128), BF16),
        ),
        in_specs=[hbm] * 13,
        out_specs=(hbm,) * 4,
        scratch_shapes=[
            m((1, 1), F32), m((1, 1), jnp.int32), m((1, 1), F32), m((1, 1), jnp.int32),
            v((24, 128), BF16), v((24, 128), BF16), v((24, 128), BF16), v((24, 128), BF16),
            v((6, 128 * J), BF16), v((6, 128 * J), BF16),
            v((NT, XY, 128), BF16),
            v((4, XY, 128), F32),
            v((4, ROWS, 128), F32),
            v((4, ROWS, 128), BF16),
            v((128, 2 * ROWS), BF16),
            v((ROWS, 256), BF16),
            v((2 * ROWS, 128), BF16),
            v((128 * J, 256), BF16),
            v((128, 128 * J), BF16),
            v((128, 128 * J), BF16),
            v((GCH, 128), F32),
            v((NZ * GCH, 128), BF16),
            v((8, GCH, 128), F32),
            v((J, 48, 128), F32),
            v((J, 48, 128), F32),
            v((FLAT, 128), F32),
            v((FLAT, 128), F32),
            v((FLAT, 128), BF16),
            v((FLAT, 128), BF16),
            v((FLAT, 128), F32),
            v((FLAT, 128), BF16),
            v((3, NK, CH, 128), BF16),
            v((2, 4, CH, 128), BF16),
            v((2, 4, CH, 128), BF16),
            v((FLAT, 128), BF16),
            v((FLAT, 256), BF16),
            v((FLAT, 256), BF16),
            v((2, ROWS, 128), F32),
            v((NT, 24, 128), F32),
            v((NT, 24, 128), F32),
            v((2, 24, 128), F32),
            v((24, 128), BF16),
            v((128, 128 * J), BF16),
            v((128, 128 * J), BF16),
            v((128 * J, 128), BF16),
            dma((10,)), dma((7,)),
            dma((3,)), dma((3,)),
            dma((NT - 1,)), dma((NT - 1,)),
            dma((NZ // 2 - 1,)), dma((NZ // 2 - 1,)),
            dma((NZ // 2,)), dma((NZ // 2,)),
            dma((3, NK)), dma((3, NK)),
            dma((2, 4)), dma((2, 4)),
            dma((NK - 1,)), dma((NK - 1,)),
            dma((3, NK)), dma((3, NK)),
            dma((NZ,)), dma((NZ,)),
            dma((NT - 1,)), dma((NT - 1,)),
        ],
        compiler_params=pltpu.CompilerParams(
            collective_id=0, has_side_effects=True, vmem_limit_bytes=63 * 1024 * 1024
        ),
        cost_estimate=pl.CostEstimate(
            flops=1_200_000_000, bytes_accessed=8_000_000, transcendentals=400_000
        ),
    )(
        x_scale, x_outlier, g_scale, g_outlier, x_quant, x_correction, g_quant, g_correction,
        gate_pre, up_pre, w_down, w_gate, w_up,
    )
    return deliver(*results)


def solution(mesh):
    both = P("tensor", "dp")
    return jax.shard_map(
        on_device,
        mesh=mesh,
        in_specs=(both,) * 8 + (P("dp", "tensor"),) * 4 + (both,),
        out_specs=(both, P("dp", "tensor"), P("dp", "tensor"), both),
        check_vma=False,
    )
```

```python
import jax
import jax.numpy as jnp
from jax import lax
from jax.experimental import pallas as pl
from jax.experimental.pallas import tpu as pltpu
from jax.sharding import PartitionSpec as P

MESH = pl.DeviceIdType.MESH
F32, BF16 = jnp.float32, jnp.bfloat16

NZ, STRIDE = 32, 4
NK = NZ // STRIDE
NT = 16
J = 13
ROWS = 192
CH = 80
FLAT = NZ * CH
CLS = NK * CH
GCH = 2 * CH
XY = 48


def rows_of(start, size, align=16):
    return pl.ds(pl.multiple_of(start, align), size)


def kernel(
    xs_in, xo_in, gs_in, go_in, xq_in, xc_in, gq_in, gc_in, gate_in, up_in, wd, wg, wu,
    gin, dgate, dup, ddown,
    xs, xo, gs, go, xq, xc, gq, gc, gate, up,
    xyb, tmp48, u4, xg, xot, og2, ogall, wd2, wgv, wuv,
    gpack, gbuf, tt, tg, tu, coef_a, coef_b, hid_o, hid_s,
    hf, hp, r1b, r2s, r2r, ha,
    gu_o, gu_s, part, rs_src, rs_dst, fin, o_in, o_gate, o_up, o_down,
    in_sem, loc_sem, sib_s, sib_r, xy_s, xy_r, gch_s, gch_r, glo_s, glo_r,
    r1_s, r1_r, r2_s, r2_r, a1_s, a1_r, a2_s, a2_r, gu_ss, gu_rs, rs_s, rs_r,
):
    dp, t = lax.axis_index("dp"), lax.axis_index("tensor")
    z, c = dp // 2, lax.rem(dp, 2)
    k0, cls = z // STRIDE, lax.rem(z, STRIDE)

    def zdev(d):
        return (lax.rem(dp + 2 * d + 2 * NZ, 2 * NZ), t)

    def tdev(i):
        return (dp, lax.rem(t + i, NT))

    sib = (dp + 1 - 2 * c, t)

    def rcopy(src, dst, ss, rs, dev):
        return pltpu.make_async_remote_copy(
            src_ref=src, dst_ref=dst, send_sem=ss, recv_sem=rs, device_id=dev, device_id_type=MESH
        )

    barrier = pltpu.get_barrier_semaphore()
    peers = [zdev(d) for d in (1, -1, 2, -2, 4, -4, 8, -8)]
    peers += [sib] + [tdev(i) for i in range(1, NT)]
    for peer in peers:
        pl.semaphore_signal(barrier, inc=1, device_id=peer, device_id_type=MESH)

    loc = [
        pltpu.make_async_copy(wd, wd2.at[:, pl.ds(0, 128)], loc_sem.at[0]),
        pltpu.make_async_copy(wg, wgv, loc_sem.at[1]),
        pltpu.make_async_copy(wu, wuv, loc_sem.at[2]),
    ]
    small = [
        pltpu.make_async_copy(src, dst, in_sem.at[n])
        for n, (src, dst) in enumerate(
            (
                (xq_in, xq), (xc_in, xc), (gq_in, gq), (gc_in, gc), (xs_in, xs), (xo_in, xo),
                (gs_in, gs), (go_in, go), (gate_in, gate), (up_in, up),
            )
        )
    ]
    for copy in small + loc:
        copy.start()
    for copy in small:
        copy.wait()

    fin[0] = xs[0, 0] * xq[...].astype(F32) + xo[0, 0].astype(F32) * xc[...].astype(F32)
    fin[1] = gs[0, 0] * gq[...].astype(F32) + go[0, 0].astype(F32) * gc[...].astype(F32)
    for a in range(2):
        for p in range(2):
            for h in range(2):
                tmp48[0, 24 * a + 12 * p + 6 * h : 24 * a + 12 * p + 6 * h + 6, :] = fin[
                    a, 12 * h + 6 * p : 12 * h + 6 * p + 6, :
                ]
    xyb[t] = tmp48[0].astype(BF16)

    def near(d):
        return lax.rem(cls + d + STRIDE, STRIDE)

    def k_of(d):
        return lax.rem(z + d + NZ, NZ) // STRIDE

    class Gather:
        def __init__(self, buf, ch, stride, towards, links, chain_s, chain_r, local_s, local_r):
            self.ch, self.stride, self.towards = ch, stride, towards
            self.nk = nk = NZ // stride
            half = nk // 2
            self.which = tuple(range(0, -half - 1, -1)) + tuple(range(1, half))

            def slot(n):
                return buf.at[self.rows(0, n)]

            self.links = [
                rcopy(slot(n), slot(n), chain_s.at[at], chain_r.at[at], zdev(d))
                for at, (n, d) in enumerate(links)
            ]
            self.local = []
            for n in range(nk):
                if towards:
                    self.local.append(
                        [
                            rcopy(slot(n), slot(n), local_s.at[m, n], local_r.at[m, n], zdev(d))
                            for m, d in enumerate(towards)
                        ]
                    )
                else:
                    at = self.index(0, n)
                    to = (lax.rem(dp + 2 - 4 * lax.rem(at, 2) + 2 * NZ, 2 * NZ), t)
                    self.local.append(
                        [rcopy(slot(n), slot(n), local_s.at[n], local_r.at[at], to)]
                    )
            self.all = self.links + sum(self.local, [])

        def index(self, d, n):
            return lax.rem(lax.rem(z + d + NZ, NZ) // self.stride + self.which[n] + self.nk, self.nk)

        def rows(self, d, n):
            cls_at = lax.rem(lax.rem(z, self.stride) + d + self.stride, self.stride)
            return rows_of(self.ch * (self.nk * cls_at + self.index(d, n)), self.ch)

        def send(self, *links):
            for at in links:
                self.links[at].start()

        def spread(self, *chunks):
            for n in chunks:
                for copy in self.local[n]:
                    copy.start()

        def arrive(self, n):
            for copy in self.local[n]:
                copy.wait_recv()

    gpack[...] = jnp.zeros_like(gpack)
    gate_val, up_val = gate[...].astype(F32), up[...].astype(F32)
    for j in range(J):
        gpack[6 * j : 6 * j + 6, :] = gate_val[:, 128 * j : 128 * j + 128]
        gpack[CH + 6 * j : CH + 6 * j + 6, :] = up_val[:, 128 * j : 128 * j + 128]

    saved = Gather(
        gbuf, GCH, 2, (), [(n, 2) for n in range(8)] + [(8 + n if n else 0, -2) for n in range(7)],
        gch_s, gch_r, glo_s, glo_r,
    )

    def saved_step(i):
        saved.links[i - 1].wait_recv()
        if i < 8:
            saved.send(i)
            saved.links[7 + i].wait_recv()
        if i < 7:
            saved.send(8 + i)
        saved.spread(i)
        if i < 8:
            saved.spread(8 + i)

    gbuf[saved.rows(0, 0), :] = gpack[...].astype(BF16)
    pl.semaphore_wait(barrier, len(peers))

    xy = [
        rcopy(xyb.at[t], xyb.at[t], xy_s.at[i - 1], xy_r.at[i - 1], tdev(i))
        for i in (10, 5, 6, 7, 9, 11, 2, 8, 14, 13, 3, 1, 15, 4, 12)
    ]
    for copy in xy:
        copy.start()
    wd_copy = rcopy(wd, wd2.at[:, pl.ds(128, 128)], sib_s.at[0], sib_r.at[0], sib)
    wd_copy.start()

    saved.send(0, 8)
    saved.spread(0)

    saved_step(1)
    for copy in xy:
        copy.wait_recv()
    for i in range(NT):
        tmp48[i % 4] = xyb[i].astype(F32)
        for a in range(4):
            u4[a, 12 * i : 12 * i + 12, :] = tmp48[i % 4, 12 * a : 12 * a + 12, :]
    for a in range(4):
        xg[a] = u4[a].astype(BF16)
    og_copy = rcopy(xg.at[3 - c], og2.at[:, pl.ds(128, 128)], sib_s.at[1], sib_r.at[1], sib)
    og_copy.start()
    og2[:, 0:128] = xg[2 + c]
    ogall[0:ROWS, :] = xg[2 + c]
    ogall[ROWS : 2 * ROWS, :] = xg[3 - c]
    tx = jnp.concatenate([u4[c], u4[1 - c]], axis=0)
    xot[...] = jnp.transpose(tx).astype(BF16)
    loc[0].wait()
    wd_copy.wait_recv()
    og_copy.wait_recv()
    saved_step(2)

    hp[J * ROWS : FLAT, :] = jnp.zeros((FLAT - J * ROWS, 128), BF16)
    hf[J * ROWS : FLAT, :] = jnp.zeros((FLAT - J * ROWS, 128), F32)
    og_val = og2[...]
    for j in range(J):
        val = lax.dot_general(
            og_val, wd2[128 * j : 128 * j + 128, :], (((1,), (1,)), ((), ())),
            preferred_element_type=F32,
        )
        hf[ROWS * j : ROWS * (j + 1), :] = val
        hp[ROWS * j : ROWS * (j + 1), :] = val.astype(BF16)

    r1 = {}
    for off in (4, 3, 5, 1, 7, 2, 6, 0):
        for n, d in enumerate((1, -1, 2)):
            base = CLS * near(d) + CH * lax.rem(k_of(d) + off, NK)
            r1[off, n] = rcopy(
                hp.at[rows_of(base, CH)], r1b.at[n, off], r1_s.at[n, off], r1_r.at[n, off], zdev(d)
            )
            r1[off, n].start()

    def window_sum(off):
        total = hf[rows_of(CLS * cls + CH * lax.rem(k0 + off, NK), CH), :]
        for n in range(3):
            r1[off, n].wait_recv()
            total = total + r1b[n, off].astype(F32)
        return total

    saved_step(3)
    r2 = []

    def pass_on(total, d):
        m = len(r2)
        r2s[m] = total.astype(BF16)
        r2.append(rcopy(r2s.at[m], r2r.at[m], r2_s.at[m], r2_r.at[m], zdev(d)))
        r2[m].start()

    def passed(m):
        r2[m].wait_recv()
        return r2r[m].astype(F32)

    pass_on(window_sum(4), 8)
    pass_on(window_sum(3), 4)
    pass_on(window_sum(5), -4)
    saved_step(4)
    pass_on(window_sum(1), 4)
    pass_on(window_sum(7), -4)
    saved_step(5)
    right, left = window_sum(2), window_sum(6)
    left = left + passed(2)
    pass_on(left, -8)
    right = right + passed(1)
    right = right + passed(0)
    pass_on(right, 8)
    total = window_sum(0)
    total = total + passed(3)
    total = total + passed(4)
    saved_step(6)
    total = total + passed(5)
    total = total + passed(6)
    back = Gather(
        ha, CH, STRIDE, (1, -1, -2),
        [(0, 4), (0, -4), (0, 8), (0, -8), (2, 4), (2, 8), (6, -4)],
        a1_s, a1_r, a2_s, a2_r,
    )
    ha[back.rows(0, 0), :] = total.astype(BF16)
    back.send(2, 3, 0, 1)
    back.spread(0)
    saved_step(7)
    back.links[0].wait_recv()
    back.links[1].wait_recv()
    back.spread(1, 5)
    saved_step(8)
    back.links[2].wait_recv()
    back.send(5, 4)
    back.links[3].wait_recv()
    back.send(6)
    back.spread(2, 6)

    for n in range(NZ // 2):
        saved.arrive(n)
    coef_a[J * ROWS : FLAT, :] = jnp.zeros((FLAT - J * ROWS, 128), F32)
    coef_b[J * ROWS : FLAT, :] = jnp.zeros((FLAT - J * ROWS, 128), F32)

    def factors(m, _):
        for q in range(8):
            start = GCH * (NZ // 2 * (q % 2) + q // 2 + 4 * m)
            tt[q] = gbuf[rows_of(start, GCH), :].astype(F32)
            for j in range(J):
                tg[j, 6 * q : 6 * q + 6, :] = tt[q, 6 * j : 6 * j + 6, :]
                tu[j, 6 * q : 6 * q + 6, :] = tt[q, CH + 6 * j : CH + 6 * j + 6, :]

        def tile(j, _):
            g, u = tg[j], tu[j]
            s = 1.0 / (1.0 + jnp.exp(-g))
            silu = g * s
            at = rows_of(ROWS * j + 48 * m, 48)
            hid_o[at, :] = (silu * u).astype(BF16)
            coef_a[at, :] = silu
            coef_b[at, :] = u * s * (1.0 + g * (1.0 - s))
            return 0

        lax.fori_loop(0, J, tile, 0)
        return 0

    lax.fori_loop(0, 4, factors, 0)
    hid_copy = rcopy(hid_o, hid_s, sib_s.at[2], sib_r.at[2], sib)
    hid_copy.start()
    gu = []

    def grads(d, n):
        at = back.rows(d, n)
        h = ha[at, :].astype(F32)
        gu_o[at, 0:128] = (h * coef_b[at, :]).astype(BF16)
        gu_o[at, 128:256] = (h * coef_a[at, :]).astype(BF16)
        m = len(gu)
        gu.append(rcopy(gu_o.at[at], gu_s.at[at], gu_ss.at[m], gu_rs.at[m], sib))
        gu[m].start()

    def arrived(n):
        for m, d in enumerate(back.towards):
            back.local[n][m].wait_recv()
            grads(-d, n)

    for n in (0, 1, 5, 2, 6):
        grads(0, n)
    arrived(0)
    arrived(1)
    arrived(5)
    hid_copy.wait_recv()

    def down(j, _):
        at = rows_of(ROWS * j, ROWS)
        both = jnp.concatenate([hid_o[at, :], hid_s[at, :]], axis=0)
        val = lax.dot_general(
            both, ogall[...], (((0,), (0,)), ((), ())), preferred_element_type=F32
        )
        o_down[rows_of(128 * j, 128), :] = val.astype(BF16)
        return 0

    lax.fori_loop(0, J, down, 0)

    outs = [pltpu.make_async_copy(o_down, ddown, loc_sem.at[3])]
    outs[0].start()

    back.links[4].wait_recv()
    back.spread(3)
    back.links[6].wait_recv()
    back.spread(7)
    grads(0, 3)
    grads(0, 7)
    arrived(2)
    arrived(6)
    back.links[5].wait_recv()
    back.spread(4)
    grads(0, 4)
    arrived(3)
    arrived(7)
    arrived(4)

    loc[1].wait()
    loc[2].wait()

    def input_part(buf):
        acc = jnp.zeros((ROWS, 128), F32)
        for j in range(J):
            w = jnp.concatenate(
                [wgv[:, 128 * j : 128 * j + 128], wuv[:, 128 * j : 128 * j + 128]], axis=1
            )
            acc = acc + lax.dot_general(
                buf[ROWS * j : ROWS * (j + 1), :], w, (((1,), (1,)), ((), ())),
                preferred_element_type=F32,
            )
        return acc

    part[c] = input_part(gu_o)
    for copy in gu:
        copy.wait_recv()
    part[1 - c] = input_part(gu_s)
    for i in range(NT):
        for p in range(2):
            rs_src[i, 12 * p : 12 * p + 12, :] = part[p, 12 * i : 12 * i + 12, :]
    rs = [
        rcopy(
            rs_src.at[lax.rem(t + i, NT)], rs_dst.at[t], rs_s.at[i - 1], rs_r.at[i - 1], tdev(i)
        )
        for i in (10, 5, 6, 7, 9, 11, 2, 8, 14, 13, 3, 1, 15, 4, 12)
    ]
    for copy in rs:
        copy.start()
    rs_dst[t] = rs_src[t]

    for j in range(J):
        both = jnp.concatenate(
            [gu_o[ROWS * j : ROWS * (j + 1), :], gu_s[ROWS * j : ROWS * (j + 1), :]], axis=0
        )
        val = jnp.dot(xot[...], both, preferred_element_type=F32).astype(BF16)
        o_gate[:, 128 * j : 128 * j + 128] = val[:, 0:128]
        o_up[:, 128 * j : 128 * j + 128] = val[:, 128:256]
    outs.append(pltpu.make_async_copy(o_gate, dgate, loc_sem.at[4]))
    outs.append(pltpu.make_async_copy(o_up, dup, loc_sem.at[5]))
    outs[1].start()
    outs[2].start()

    sends = xy + [wd_copy, og_copy, hid_copy] + saved.all + back.all + gu
    sends += list(r1.values()) + r2
    for copy in sends:
        copy.wait_send()
    for copy in rs:
        copy.wait()
    total = rs_dst[0]
    for i in range(1, NT):
        total = total + rs_dst[i]
    fin[0] = total
    for p in range(2):
        for h in range(2):
            fin[1, 12 * h + 6 * p : 12 * h + 6 * p + 6, :] = fin[
                0, 12 * p + 6 * h : 12 * p + 6 * h + 6, :
            ]
    o_in[...] = fin[1].astype(BF16)
    outs.append(pltpu.make_async_copy(o_in, gin, loc_sem.at[6]))
    outs[3].start()
    for copy in outs:
        copy.wait()


def deliver_kernel(*refs):
    srcs, dsts, bufs, sem = refs[:4], refs[4:8], refs[8:12], refs[12]
    order = (1, 2, 3, 0)
    ins = [pltpu.make_async_copy(srcs[n], bufs[n], sem.at[0, n]) for n in order]
    outs = [pltpu.make_async_copy(bufs[n], dsts[n], sem.at[1, n]) for n in order]
    for copy in ins:
        copy.start()
    for n in range(4):
        ins[n].wait()
        outs[n].start()
    for copy in outs:
        copy.wait()


def deliver(*results):
    hbm = pl.BlockSpec(memory_space=pltpu.HBM)
    return pl.pallas_call(
        deliver_kernel,
        name="deliver",
        out_shape=tuple(jax.ShapeDtypeStruct(r.shape, r.dtype) for r in results),
        in_specs=[hbm] * 4,
        out_specs=(hbm,) * 4,
        scratch_shapes=[pltpu.VMEM(r.shape, r.dtype) for r in results]
        + [pltpu.SemaphoreType.DMA((2, 4))],
        compiler_params=pltpu.CompilerParams(vmem_limit_bytes=63 * 1024 * 1024),
    )(*results)


def on_device(
    x_quant, x_scale, x_outlier, x_correction, g_quant, g_scale, g_outlier, g_correction,
    gate_pre, up_pre, w_gate, w_up, w_down,
):
    hbm = pl.BlockSpec(memory_space=pltpu.HBM)
    v, m, dma = pltpu.VMEM, pltpu.SMEM, pltpu.SemaphoreType.DMA
    results = pl.pallas_call(
        kernel,
        name="ffn_backward",
        out_shape=(
            jax.ShapeDtypeStruct((24, 128), BF16),
            jax.ShapeDtypeStruct((128, 128 * J), BF16),
            jax.ShapeDtypeStruct((128, 128 * J), BF16),
            jax.ShapeDtypeStruct((128 * J, 128), BF16),
        ),
        in_specs=[hbm] * 13,
        out_specs=(hbm,) * 4,
        scratch_shapes=[
            m((1, 1), F32), m((1, 1), jnp.int32), m((1, 1), F32), m((1, 1), jnp.int32),
            v((24, 128), BF16), v((24, 128), BF16), v((24, 128), BF16), v((24, 128), BF16),
            v((6, 128 * J), BF16), v((6, 128 * J), BF16),
            v((NT, XY, 128), BF16),
            v((4, XY, 128), F32),
            v((4, ROWS, 128), F32),
            v((4, ROWS, 128), BF16),
            v((128, 2 * ROWS), BF16),
            v((ROWS, 256), BF16),
            v((2 * ROWS, 128), BF16),
            v((128 * J, 256), BF16),
            v((128, 128 * J), BF16),
            v((128, 128 * J), BF16),
            v((GCH, 128), F32),
            v((NZ * GCH, 128), BF16),
            v((8, GCH, 128), F32),
            v((J, 48, 128), F32),
            v((J, 48, 128), F32),
            v((FLAT, 128), F32),
            v((FLAT, 128), F32),
            v((FLAT, 128), BF16),
            v((FLAT, 128), BF16),
            v((FLAT, 128), F32),
            v((FLAT, 128), BF16),
            v((3, NK, CH, 128), BF16),
            v((7, CH, 128), BF16),
            v((7, CH, 128), BF16),
            v((FLAT, 128), BF16),
            v((FLAT, 256), BF16),
            v((FLAT, 256), BF16),
            v((2, ROWS, 128), F32),
            v((NT, 24, 128), F32),
            v((NT, 24, 128), F32),
            v((2, 24, 128), F32),
            v((24, 128), BF16),
            v((128, 128 * J), BF16),
            v((128, 128 * J), BF16),
            v((128 * J, 128), BF16),
            dma((10,)), dma((7,)),
            dma((3,)), dma((3,)),
            dma((NT - 1,)), dma((NT - 1,)),
            dma((NZ // 2 - 1,)), dma((NZ // 2 - 1,)),
            dma((NZ // 2,)), dma((NZ // 2,)),
            dma((3, NK)), dma((3, NK)),
            dma((7,)), dma((7,)),
            dma((NK - 1,)), dma((NK - 1,)),
            dma((3, NK)), dma((3, NK)),
            dma((NZ,)), dma((NZ,)),
            dma((NT - 1,)), dma((NT - 1,)),
        ],
        compiler_params=pltpu.CompilerParams(
            collective_id=0, has_side_effects=True, vmem_limit_bytes=63 * 1024 * 1024
        ),
        cost_estimate=pl.CostEstimate(
            flops=1_200_000_000, bytes_accessed=8_000_000, transcendentals=400_000
        ),
    )(
        x_scale, x_outlier, g_scale, g_outlier, x_quant, x_correction, g_quant, g_correction,
        gate_pre, up_pre, w_down, w_gate, w_up,
    )
    return deliver(*results)


def solution(mesh):
    both = P("tensor", "dp")
    return jax.shard_map(
        on_device,
        mesh=mesh,
        in_specs=(both,) * 8 + (P("dp", "tensor"),) * 4 + (both,),
        out_specs=(both, P("dp", "tensor"), P("dp", "tensor"), both),
        check_vma=False,
    )
```

```python
import jax
import jax.numpy as jnp
from jax import lax
from jax.experimental import pallas as pl
from jax.experimental.pallas import tpu as pltpu
from jax.sharding import PartitionSpec as P

MESH = pl.DeviceIdType.MESH
F32, BF16 = jnp.float32, jnp.bfloat16

NZ, STRIDE = 32, 4
NK = NZ // STRIDE
NT = 16
J = 13
ROWS = 192
CH = 80
FLAT = NZ * CH
CLS = NK * CH
GCH = 2 * CH
XY = 48


def rows_of(start, size, align=16):
    return pl.ds(pl.multiple_of(start, align), size)


def kernel(
    xs_in, xo_in, gs_in, go_in, xq_in, xc_in, gq_in, gc_in, gate_in, up_in, wd, wg, wu,
    gin, dgate, dup, ddown,
    xs, xo, gs, go, xq, xc, gq, gc, gate, up,
    xyb, tmp48, u4, xg, xot, og2, ogall, wd2, wgv, wuv,
    gpack, gbuf, tt, tg, tu, coef_a, coef_b, hid_o, hid_s,
    hf, hp, r1b, r2s, r2r, ha,
    gu_o, gu_s, part, rs_src, rs_dst, fin, o_in, o_gate, o_up, o_down,
    in_sem, loc_sem, sib_s, sib_r, xy_s, xy_r, gch_s, gch_r, glo_s, glo_r,
    r1_s, r1_r, r2_s, r2_r, a1_s, a1_r, a2_s, a2_r, gu_ss, gu_rs, rs_s, rs_r,
):
    dp, t = lax.axis_index("dp"), lax.axis_index("tensor")
    z, c = dp // 2, lax.rem(dp, 2)
    k0, cls = z // STRIDE, lax.rem(z, STRIDE)

    def zdev(d):
        return (lax.rem(dp + 2 * d + 2 * NZ, 2 * NZ), t)

    def tdev(i):
        return (dp, lax.rem(t + i, NT))

    sib = (dp + 1 - 2 * c, t)

    def rcopy(src, dst, ss, rs, dev):
        return pltpu.make_async_remote_copy(
            src_ref=src, dst_ref=dst, send_sem=ss, recv_sem=rs, device_id=dev, device_id_type=MESH
        )

    barrier = pltpu.get_barrier_semaphore()
    peers = [zdev(d) for d in (1, -1, 2, -2, STRIDE, -STRIDE)]
    peers += [sib] + [tdev(i) for i in range(1, NT)]
    for peer in peers:
        pl.semaphore_signal(barrier, inc=1, device_id=peer, device_id_type=MESH)

    loc = [
        pltpu.make_async_copy(wd, wd2.at[:, pl.ds(0, 128)], loc_sem.at[0]),
        pltpu.make_async_copy(wg, wgv, loc_sem.at[1]),
        pltpu.make_async_copy(wu, wuv, loc_sem.at[2]),
    ]
    small = [
        pltpu.make_async_copy(src, dst, in_sem.at[n])
        for n, (src, dst) in enumerate(
            (
                (xq_in, xq), (xc_in, xc), (gq_in, gq), (gc_in, gc), (xs_in, xs), (xo_in, xo),
                (gs_in, gs), (go_in, go), (gate_in, gate), (up_in, up),
            )
        )
    ]
    for copy in small + loc:
        copy.start()
    for copy in small:
        copy.wait()

    fin[0] = xs[0, 0] * xq[...].astype(F32) + xo[0, 0].astype(F32) * xc[...].astype(F32)
    fin[1] = gs[0, 0] * gq[...].astype(F32) + go[0, 0].astype(F32) * gc[...].astype(F32)
    for a in range(2):
        for p in range(2):
            for h in range(2):
                tmp48[0, 24 * a + 12 * p + 6 * h : 24 * a + 12 * p + 6 * h + 6, :] = fin[
                    a, 12 * h + 6 * p : 12 * h + 6 * p + 6, :
                ]
    xyb[t] = tmp48[0].astype(BF16)

    def near(d):
        return lax.rem(cls + d + STRIDE, STRIDE)

    def k_of(d):
        return lax.rem(z + d + NZ, NZ) // STRIDE

    class Gather:
        def __init__(self, buf, ch, stride, towards, chain_s, chain_r, local_s, local_r):
            self.ch, self.stride, self.towards = ch, stride, towards
            self.nk = nk = NZ // stride
            self.half = half = nk // 2
            self.which = tuple(range(0, -half - 1, -1)) + tuple(range(1, half))

            def slot(n):
                return buf.at[self.rows(0, n)]

            def link(n, at, d):
                return rcopy(slot(n), slot(n), chain_s.at[at], chain_r.at[at], zdev(d))

            self.right = [link(n, n, stride) for n in range(half)]
            self.left = [link(half + n if n else 0, half + n, -stride) for n in range(half - 1)]
            self.local, self.across = [], []
            for n in range(nk):
                if towards:
                    odd = lax.rem(self.index(0, n), 2)
                    to = (lax.rem(dp + 8 * odd - 4 + 2 * NZ, 2 * NZ), t)
                    at = lax.rem(self.which[n] + 2 * nk - odd, nk)
                    self.local.append(
                        [
                            rcopy(slot(n), slot(n), local_s.at[m, n], local_r.at[m, n], zdev(d))
                            for m, d in enumerate(towards)
                        ]
                        + [rcopy(slot(n), slot(n), local_s.at[2, n], local_r.at[2, at], to)]
                    )
                    self.across.append(
                        rcopy(slot(n), slot(n), local_s.at[2, n], local_r.at[2, self.which[n] % nk], to)
                    )
                else:
                    at = self.index(0, n)
                    to = (lax.rem(dp + 2 - 4 * lax.rem(at, 2) + 2 * NZ, 2 * NZ), t)
                    self.local.append(
                        [rcopy(slot(n), slot(n), local_s.at[n], local_r.at[at], to)]
                    )
            self.all = self.right + self.left + sum(self.local, [])

        def index(self, d, n):
            return lax.rem(lax.rem(z + d + NZ, NZ) // self.stride + self.which[n] + self.nk, self.nk)

        def rows(self, d, n):
            cls_at = lax.rem(lax.rem(z, self.stride) + d + self.stride, self.stride)
            return rows_of(self.ch * (self.nk * cls_at + self.index(d, n)), self.ch)

        def begin(self):
            self.right[0].start()
            self.left[0].start()
            self.spread(0)

        def spread(self, n):
            for copy in self.local[n]:
                copy.start()

        def step(self, i):
            half = self.half
            self.right[i - 1].wait_recv()
            if i < half:
                self.right[i].start()
                self.left[i - 1].wait_recv()
            if i < half - 1:
                self.left[i].start()
            self.spread(i)
            if i < half:
                self.spread(half + i)

        def arrive(self, n):
            for copy in self.local[n]:
                copy.wait_recv()

    gpack[...] = jnp.zeros_like(gpack)
    gate_val, up_val = gate[...].astype(F32), up[...].astype(F32)
    for j in range(J):
        gpack[6 * j : 6 * j + 6, :] = gate_val[:, 128 * j : 128 * j + 128]
        gpack[CH + 6 * j : CH + 6 * j + 6, :] = up_val[:, 128 * j : 128 * j + 128]

    saved = Gather(gbuf, GCH, 2, (), gch_s, gch_r, glo_s, glo_r)
    gbuf[saved.rows(0, 0), :] = gpack[...].astype(BF16)
    pl.semaphore_wait(barrier, len(peers))

    xy = [
        rcopy(xyb.at[t], xyb.at[t], xy_s.at[i - 1], xy_r.at[i - 1], tdev(i))
        for i in (10, 5, 6, 7, 9, 11, 2, 8, 14, 13, 3, 1, 15, 4, 12)
    ]
    for copy in xy:
        copy.start()
    wd_copy = rcopy(wd, wd2.at[:, pl.ds(128, 128)], sib_s.at[0], sib_r.at[0], sib)
    wd_copy.start()

    saved.begin()

    saved.step(1)
    for copy in xy:
        copy.wait_recv()
    for i in range(NT):
        tmp48[i % 4] = xyb[i].astype(F32)
        for a in range(4):
            u4[a, 12 * i : 12 * i + 12, :] = tmp48[i % 4, 12 * a : 12 * a + 12, :]
    for a in range(4):
        xg[a] = u4[a].astype(BF16)
    og_copy = rcopy(xg.at[3 - c], og2.at[:, pl.ds(128, 128)], sib_s.at[1], sib_r.at[1], sib)
    og_copy.start()
    og2[:, 0:128] = xg[2 + c]
    ogall[0:ROWS, :] = xg[2 + c]
    ogall[ROWS : 2 * ROWS, :] = xg[3 - c]
    tx = jnp.concatenate([u4[c], u4[1 - c]], axis=0)
    xot[...] = jnp.transpose(tx).astype(BF16)
    loc[0].wait()
    wd_copy.wait_recv()
    og_copy.wait_recv()
    saved.step(2)

    hp[J * ROWS : FLAT, :] = jnp.zeros((FLAT - J * ROWS, 128), BF16)
    hf[J * ROWS : FLAT, :] = jnp.zeros((FLAT - J * ROWS, 128), F32)
    og_val = og2[...]
    for j in range(J):
        val = lax.dot_general(
            og_val, wd2[128 * j : 128 * j + 128, :], (((1,), (1,)), ((), ())),
            preferred_element_type=F32,
        )
        hf[ROWS * j : ROWS * (j + 1), :] = val
        hp[ROWS * j : ROWS * (j + 1), :] = val.astype(BF16)

    r1, r1_in = {}, {}
    for off in (4, 5, 3, 6, 2, 7, 1, 0):
        for n, d in enumerate((1, -1, 2)):
            k = lax.rem(k_of(d) + off, NK)
            to, at = zdev(d), off
            if n == 2:
                odd = lax.rem(k, 2)
                to = (lax.rem(dp + 4 - 8 * odd + 2 * NZ, 2 * NZ), t)
                at = lax.rem(off + odd, NK)
            src = hp.at[rows_of(CLS * near(d) + CH * k, CH)]
            r1[off, n] = rcopy(src, r1b.at[n, at], r1_s.at[n, off], r1_r.at[n, at], to)
            r1_in[off, n] = rcopy(src, r1b.at[n, off], r1_s.at[n, off], r1_r.at[n, off], to)
            r1[off, n].start()

    def window_sum(off):
        total = hf[rows_of(CLS * cls + CH * lax.rem(k0 + off, NK), CH), :]
        for n in range(3):
            r1_in[off, n].wait_recv()
            total = total + r1b[n, off].astype(F32)
        return total

    saved.step(3)
    r2 = {}
    for i in range(1, 5):
        for w, off, d in ((0, 5 - i, STRIDE), (1, 4 + i, -STRIDE)):
            if w == 1 and i == 4:
                continue
            total = window_sum(off)
            if i > 1:
                r2[w, i - 1].wait_recv()
                total = total + r2r[w, i - 2].astype(F32)
            r2s[w, i - 1] = total.astype(BF16)
            r2[w, i] = rcopy(
                r2s.at[w, i - 1], r2r.at[w, i - 1], r2_s.at[w, i - 1], r2_r.at[w, i - 1], zdev(d)
            )
            r2[w, i].start()
        saved.step(3 + i)
    total = window_sum(0)
    r2[1, 3].wait_recv()
    total = total + r2r[1, 2].astype(F32)
    r2[0, 4].wait_recv()
    total = total + r2r[0, 3].astype(F32)
    back = Gather(ha, CH, STRIDE, (1, -1), a1_s, a1_r, a2_s, a2_r)
    ha[back.rows(0, 0), :] = total.astype(BF16)
    back.begin()
    saved.step(8)

    back.step(1)
    for n in range(NZ // 2):
        saved.arrive(n)
    coef_a[J * ROWS : FLAT, :] = jnp.zeros((FLAT - J * ROWS, 128), F32)
    coef_b[J * ROWS : FLAT, :] = jnp.zeros((FLAT - J * ROWS, 128), F32)

    def factors(m, _):
        for q in range(8):
            start = GCH * (NZ // 2 * (q % 2) + q // 2 + 4 * m)
            tt[q] = gbuf[rows_of(start, GCH), :].astype(F32)
            for j in range(J):
                tg[j, 6 * q : 6 * q + 6, :] = tt[q, 6 * j : 6 * j + 6, :]
                tu[j, 6 * q : 6 * q + 6, :] = tt[q, CH + 6 * j : CH + 6 * j + 6, :]

        def tile(j, _):
            g, u = tg[j], tu[j]
            s = 1.0 / (1.0 + jnp.exp(-g))
            silu = g * s
            at = rows_of(ROWS * j + 48 * m, 48)
            hid_o[at, :] = (silu * u).astype(BF16)
            coef_a[at, :] = silu
            coef_b[at, :] = u * s * (1.0 + g * (1.0 - s))
            return 0

        lax.fori_loop(0, J, tile, 0)
        return 0

    lax.fori_loop(0, 4, factors, 0)
    hid_copy = rcopy(hid_o, hid_s, sib_s.at[2], sib_r.at[2], sib)
    hid_copy.start()
    gu = []

    def grads(d, n):
        at = back.rows(d, n)
        h = ha[at, :].astype(F32)
        gu_o[at, 0:128] = (h * coef_b[at, :]).astype(BF16)
        gu_o[at, 128:256] = (h * coef_a[at, :]).astype(BF16)
        m = len(gu)
        gu.append(rcopy(gu_o.at[at], gu_s.at[at], gu_ss.at[m], gu_rs.at[m], sib))
        gu[m].start()

    def arrived(n):
        for m, d in enumerate(back.towards):
            back.local[n][m].wait_recv()
            grads(-d, n)
        back.across[n].wait_recv()
        grads(2, n)

    grads(0, 0)
    for n in (1, 5):
        grads(0, n)
    arrived(0)
    back.step(2)
    hid_copy.wait_recv()

    def down(j, _):
        at = rows_of(ROWS * j, ROWS)
        both = jnp.concatenate([hid_o[at, :], hid_s[at, :]], axis=0)
        val = lax.dot_general(
            both, ogall[...], (((0,), (0,)), ((), ())), preferred_element_type=F32
        )
        o_down[rows_of(128 * j, 128), :] = val.astype(BF16)
        return 0

    lax.fori_loop(0, J, down, 0)

    outs = [pltpu.make_async_copy(o_down, ddown, loc_sem.at[3])]
    outs[0].start()

    grads(0, 2)
    grads(0, 6)
    arrived(1)
    arrived(5)
    back.step(3)
    grads(0, 3)
    grads(0, 7)
    arrived(2)
    arrived(6)
    back.step(4)
    grads(0, 4)
    arrived(3)
    arrived(7)
    arrived(4)

    loc[1].wait()
    loc[2].wait()

    def input_part(buf):
        acc = jnp.zeros((ROWS, 128), F32)
        for j in range(J):
            w = jnp.concatenate(
                [wgv[:, 128 * j : 128 * j + 128], wuv[:, 128 * j : 128 * j + 128]], axis=1
            )
            acc = acc + lax.dot_general(
                buf[ROWS * j : ROWS * (j + 1), :], w, (((1,), (1,)), ((), ())),
                preferred_element_type=F32,
            )
        return acc

    part[c] = input_part(gu_o)
    for copy in gu:
        copy.wait_recv()
    part[1 - c] = input_part(gu_s)
    for i in range(NT):
        for p in range(2):
            rs_src[i, 12 * p : 12 * p + 12, :] = part[p, 12 * i : 12 * i + 12, :]
    rs = [
        rcopy(
            rs_src.at[lax.rem(t + i, NT)], rs_dst.at[t], rs_s.at[i - 1], rs_r.at[i - 1], tdev(i)
        )
        for i in (10, 5, 6, 7, 9, 11, 2, 8, 14, 13, 3, 1, 15, 4, 12)
    ]
    for copy in rs:
        copy.start()
    rs_dst[t] = rs_src[t]

    for j in range(J):
        both = jnp.concatenate(
            [gu_o[ROWS * j : ROWS * (j + 1), :], gu_s[ROWS * j : ROWS * (j + 1), :]], axis=0
        )
        val = jnp.dot(xot[...], both, preferred_element_type=F32).astype(BF16)
        o_gate[:, 128 * j : 128 * j + 128] = val[:, 0:128]
        o_up[:, 128 * j : 128 * j + 128] = val[:, 128:256]
    outs.append(pltpu.make_async_copy(o_gate, dgate, loc_sem.at[4]))
    outs.append(pltpu.make_async_copy(o_up, dup, loc_sem.at[5]))
    outs[1].start()
    outs[2].start()

    sends = xy + [wd_copy, og_copy, hid_copy] + saved.all + back.all + gu
    sends += list(r1.values()) + list(r2.values())
    for copy in sends:
        copy.wait_send()
    for copy in rs:
        copy.wait()
    total = rs_dst[0]
    for i in range(1, NT):
        total = total + rs_dst[i]
    fin[0] = total
    for p in range(2):
        for h in range(2):
            fin[1, 12 * h + 6 * p : 12 * h + 6 * p + 6, :] = fin[
                0, 12 * p + 6 * h : 12 * p + 6 * h + 6, :
            ]
    o_in[...] = fin[1].astype(BF16)
    outs.append(pltpu.make_async_copy(o_in, gin, loc_sem.at[6]))
    outs[3].start()
    for copy in outs:
        copy.wait()


def deliver_kernel(*refs):
    srcs, dsts, bufs, sem = refs[:4], refs[4:8], refs[8:12], refs[12]
    order = (1, 2, 3, 0)
    ins = [pltpu.make_async_copy(srcs[n], bufs[n], sem.at[0, n]) for n in order]
    outs = [pltpu.make_async_copy(bufs[n], dsts[n], sem.at[1, n]) for n in order]
    for copy in ins:
        copy.start()
    for n in range(4):
        ins[n].wait()
        outs[n].start()
    for copy in outs:
        copy.wait()


def deliver(*results):
    hbm = pl.BlockSpec(memory_space=pltpu.HBM)
    return pl.pallas_call(
        deliver_kernel,
        name="deliver",
        out_shape=tuple(jax.ShapeDtypeStruct(r.shape, r.dtype) for r in results),
        in_specs=[hbm] * 4,
        out_specs=(hbm,) * 4,
        scratch_shapes=[pltpu.VMEM(r.shape, r.dtype) for r in results]
        + [pltpu.SemaphoreType.DMA((2, 4))],
        compiler_params=pltpu.CompilerParams(vmem_limit_bytes=63 * 1024 * 1024),
    )(*results)


def on_device(
    x_quant, x_scale, x_outlier, x_correction, g_quant, g_scale, g_outlier, g_correction,
    gate_pre, up_pre, w_gate, w_up, w_down,
):
    hbm = pl.BlockSpec(memory_space=pltpu.HBM)
    v, m, dma = pltpu.VMEM, pltpu.SMEM, pltpu.SemaphoreType.DMA
    results = pl.pallas_call(
        kernel,
        name="ffn_backward",
        out_shape=(
            jax.ShapeDtypeStruct((24, 128), BF16),
            jax.ShapeDtypeStruct((128, 128 * J), BF16),
            jax.ShapeDtypeStruct((128, 128 * J), BF16),
            jax.ShapeDtypeStruct((128 * J, 128), BF16),
        ),
        in_specs=[hbm] * 13,
        out_specs=(hbm,) * 4,
        scratch_shapes=[
            m((1, 1), F32), m((1, 1), jnp.int32), m((1, 1), F32), m((1, 1), jnp.int32),
            v((24, 128), BF16), v((24, 128), BF16), v((24, 128), BF16), v((24, 128), BF16),
            v((6, 128 * J), BF16), v((6, 128 * J), BF16),
            v((NT, XY, 128), BF16),
            v((4, XY, 128), F32),
            v((4, ROWS, 128), F32),
            v((4, ROWS, 128), BF16),
            v((128, 2 * ROWS), BF16),
            v((ROWS, 256), BF16),
            v((2 * ROWS, 128), BF16),
            v((128 * J, 256), BF16),
            v((128, 128 * J), BF16),
            v((128, 128 * J), BF16),
            v((GCH, 128), F32),
            v((NZ * GCH, 128), BF16),
            v((8, GCH, 128), F32),
            v((J, 48, 128), F32),
            v((J, 48, 128), F32),
            v((FLAT, 128), F32),
            v((FLAT, 128), F32),
            v((FLAT, 128), BF16),
            v((FLAT, 128), BF16),
            v((FLAT, 128), F32),
            v((FLAT, 128), BF16),
            v((3, NK, CH, 128), BF16),
            v((2, 4, CH, 128), BF16),
            v((2, 4, CH, 128), BF16),
            v((FLAT, 128), BF16),
            v((FLAT, 256), BF16),
            v((FLAT, 256), BF16),
            v((2, ROWS, 128), F32),
            v((NT, 24, 128), F32),
            v((NT, 24, 128), F32),
            v((2, 24, 128), F32),
            v((24, 128), BF16),
            v((128, 128 * J), BF16),
            v((128, 128 * J), BF16),
            v((128 * J, 128), BF16),
            dma((10,)), dma((7,)),
            dma((3,)), dma((3,)),
            dma((NT - 1,)), dma((NT - 1,)),
            dma((NZ // 2 - 1,)), dma((NZ // 2 - 1,)),
            dma((NZ // 2,)), dma((NZ // 2,)),
            dma((3, NK)), dma((3, NK)),
            dma((2, 4)), dma((2, 4)),
            dma((NK - 1,)), dma((NK - 1,)),
            dma((3, NK)), dma((3, NK)),
            dma((NZ,)), dma((NZ,)),
            dma((NT - 1,)), dma((NT - 1,)),
        ],
        compiler_params=pltpu.CompilerParams(
            collective_id=0, has_side_effects=True, vmem_limit_bytes=63 * 1024 * 1024
        ),
        cost_estimate=pl.CostEstimate(
            flops=1_200_000_000, bytes_accessed=8_000_000, transcendentals=400_000
        ),
    )(
        x_scale, x_outlier, g_scale, g_outlier, x_quant, x_correction, g_quant, g_correction,
        gate_pre, up_pre, w_down, w_gate, w_up,
    )
    return deliver(*results)


def solution(mesh):
    both = P("tensor", "dp")
    return jax.shard_map(
        on_device,
        mesh=mesh,
        in_specs=(both,) * 8 + (P("dp", "tensor"),) * 4 + (both,),
        out_specs=(both, P("dp", "tensor"), P("dp", "tensor"), both),
        check_vma=False,
    )
```
